512 devices in a mesh: ctx: 16 (over z), rep: 32 (over x, y, core).
Axes of the slice: x: 4, y: 4, z: 16, core: 2. Of those that a mesh axis runs over, the one named last changes fastest.
Arguments:
- cache_keys: bfloat16 [32, 65536, 128], P('rep', 'ctx'), may hold values from -8 to 8
- cache_values: bfloat16 [32, 65536, 128], P('rep', 'ctx'), may hold values from -6 to 6
- query_pool: bfloat16 [32, 4096, 128], P('rep', 'ctx'), may hold values from -8 to 8
- kept_index: int32 [32, 4096], P('rep', 'ctx'), may hold values from 0 to 65535, as said below
- ref_index: int32 [32, 512], P('rep'), may hold values from 0 to 4095, as said below
Outputs:
- fitted_values: float32 [32, 4096, 128], P('rep', 'ctx')
The draws below stay inside these ranges and needn't reach their ends.
Inputs may be any that keep to these rules, and one draw needn't show every extreme that they name: `kept_index`: for each pair, the 256 kept slots of block c name distinct positions of cache block c, c * 4096 to (c + 1) * 4096 - 1. `ref_index`: distinct within each pair.
All inputs are finite; a program needn't handle non-finite values.
Results may differ from the reference program's by a relative error of at most 0.0003.
Values may be sent and summed in bfloat16 or wider, within the bound.
A program may use at most 64 MiB of HBM per device.

```python
import jax
import jax.numpy as jnp
from jax import lax

DH = 128
KVH = 8
CTX_DEV = 4096
KEPT_DEV = 256
NQ = 512
ITERS = 3
CTX = 65536
KEPT = 4096
POOL = 4096
REQS = 4
N_CTX = 16


def common_perms(key):
    key = jax.random.fold_in(key, 101)
    blocks = KEPT // KEPT_DEV
    pair_keys = jax.random.split(key, REQS * KVH * blocks)
    perms = jax.vmap(lambda single: jax.random.permutation(single, CTX_DEV))(pair_keys)
    return perms.reshape(REQS * KVH, blocks, CTX_DEV).astype(jnp.int32)


def common_kept(key):
    blocks = KEPT // KEPT_DEV
    picked = common_perms(key)[:, :, :KEPT_DEV]
    offsets = (jnp.arange(blocks, dtype=jnp.int32) * CTX_DEV)[None, :, None]
    return (picked + offsets).reshape(REQS * KVH, KEPT)


def common_refs(key):
    key = jax.random.fold_in(key, 102)
    pair_keys = jax.random.split(key, REQS * KVH)
    picked = jax.vmap(lambda single: jax.random.permutation(single, POOL)[:NQ])(pair_keys)
    return picked.astype(jnp.int32)


def draw_kept_index(key, part):
    return common_kept(key)


def draw_ref_index(key, part):
    return common_refs(key)


def draw_cache_keys(key, part):
    key = jax.random.fold_in(key, 1)
    base = jnp.clip(jax.random.normal(key, (REQS * KVH, CTX, DH), jnp.float32), -8.0, 8.0)
    return base.astype(jnp.bfloat16)


def draw_query_pool(key, part):
    key = jax.random.fold_in(key, 2)
    base = jnp.clip(jax.random.normal(key, (REQS * KVH, POOL, DH), jnp.float32), -8.0, 8.0)
    return base.astype(jnp.bfloat16)


def shard_levels(key, shape, cuts, smallest, largest):
    def one(dim, parts):
        steps = jax.random.uniform(jax.random.fold_in(jax.random.fold_in(key, 6), dim), (parts,), jnp.float32, smallest / len(cuts), largest / len(cuts))
        return jnp.repeat(jnp.exp(steps), shape[dim] // parts).reshape((-1,) + (1,) * (len(shape) - dim - 1))

    loudness = one(*cuts[0])
    for cut in cuts[1:]:
        loudness = loudness * one(*cut)
    return loudness


def noise(own_key, dims, deviation, reach, cuts=(), kind=jnp.bfloat16):
    gain = shard_levels(own_key, dims, cuts, -0.22, 0.18) if cuts else 1.0
    entries = jax.random.normal(own_key, dims, jnp.float32) * deviation * gain
    return jnp.minimum(jnp.maximum(entries, -reach), reach).astype(kind)


def setup_inputs(seed: int = 0) -> dict:
    arg_keys = jax.random.split(jax.random.key(seed), 6)
    return {
        "cache_keys": draw_cache_keys(jax.random.fold_in(arg_keys[5], 71), 0),
        "cache_values": noise(arg_keys[1], (REQS * KVH, CTX, DH), 1.0, 6.0, ((0, 32), (1, 16))),
        "query_pool": draw_query_pool(jax.random.fold_in(arg_keys[5], 71), 0),
        "kept_index": draw_kept_index(jax.random.fold_in(arg_keys[5], 71), 0),
        "ref_index": draw_ref_index(jax.random.fold_in(arg_keys[5], 71), 0),
    }


def one_pair(items):
    keys, values, pool, kept, refs = items
    highest = lax.Precision.HIGHEST
    scale = 1.0 / (DH ** 0.5)
    ridge = 0.3 * NQ / (KEPT * KEPT)
    queries = jnp.take(pool, refs.astype(jnp.int32), axis=0)
    key_blocks = keys.reshape(N_CTX, CTX_DEV, DH)
    value_blocks = values.reshape(N_CTX, CTX_DEV, DH)

    def shard_part(pieces):
        key_rows, value_rows = pieces
        scores = jnp.dot(queries, key_rows.T, preferred_element_type=jnp.float32) * scale
        maxima = jnp.max(scores, axis=1)
        expo = jnp.exp(scores - maxima[:, None])
        totals = jnp.sum(expo, axis=1)
        weighted = jnp.dot(expo.astype(jnp.bfloat16), value_rows, preferred_element_type=jnp.float32)
        return maxima, totals, weighted

    maxima, totals, weighted = lax.map(shard_part, (key_blocks, value_blocks))
    top = jnp.max(maxima, axis=0)
    factor = jnp.exp(maxima - top[None, :])
    target = jnp.sum(factor[:, :, None] * weighted, axis=0) / jnp.sum(factor * totals, axis=0)[:, None]
    kept_keys = jnp.take(keys, kept.astype(jnp.int32), axis=0)
    kept_vals = jnp.take(values, kept.astype(jnp.int32), axis=0).astype(jnp.float32)
    scores = jnp.dot(queries, kept_keys.T, preferred_element_type=jnp.float32) * scale
    expo = jnp.exp(scores - jnp.max(scores, axis=1, keepdims=True))
    attend = expo / jnp.sum(expo, axis=1, keepdims=True)
    fitted = kept_vals
    residual = jnp.dot(attend.T, target - jnp.dot(attend, kept_vals, precision=highest), precision=highest)
    direction = residual
    norm_now = jnp.sum(residual * residual, axis=0)
    for step in range(ITERS):
        image = jnp.dot(attend, direction, precision=highest)
        curve = jnp.sum(image * image, axis=0) + ridge * jnp.sum(direction * direction, axis=0)
        alpha = norm_now / curve
        fitted = fitted + alpha * direction
        residual = residual - alpha * (jnp.dot(attend.T, image, precision=highest) + ridge * direction)
        norm_next = jnp.sum(residual * residual, axis=0)
        direction = residual + (norm_next / norm_now) * direction
        norm_now = norm_next
    return fitted


def reference(cache_keys, cache_values, query_pool, kept_index, ref_index):
    return lax.map(one_pair, (cache_keys, cache_values, query_pool, kept_index, ref_index))
```

```python
import functools

import jax
import jax.numpy as jnp
from jax import lax
from jax.experimental import pallas as pl
from jax.experimental.pallas import tpu as pltpu
from jax.sharding import PartitionSpec as P

ITERS = 3
HALVES = 2
F32 = jnp.float32
BF16 = jnp.bfloat16
MESH = pl.DeviceIdType.MESH


def nt(a, b):
    return lax.dot_general(a, b, (((1,), (1,)), ((), ())), preferred_element_type=F32)


def nn(a, b):
    return lax.dot_general(a, b, (((1,), (0,)), ((), ())), preferred_element_type=F32)


def split(x):
    high = x.astype(BF16)
    return high, (x - high.astype(F32)).astype(BF16)


def kernel(
    n, keys_hbm, vals_hbm, pool_ref, kept_ref, ref_ref, out_ref,
    keys, vals, vals_t, q_part, q_recv, q_blk, q_all, kk, v_t, v_recv,
    s_buf, p_t, stats, p_recv, stats_recv, a_buf, top_buf, a_high, a_low, gram, res, fin,
    load_sem, q_send, q_got, g_send, g_got, ring_send, ring_got, v_send, v_got,
    p_send, p_got, st_send, st_got, f_send, f_got,
):
    me = lax.axis_index("ctx")
    rows, head = keys.shape
    kept = kk.shape[1]
    queries = q_all.shape[0]
    half = queries // HALVES
    blk = half // n
    cols = head // n
    scale = 1.0 / head**0.5
    ridge = 0.3 * queries / ((kept * n) * (kept * n))

    def peer(d):
        return {"ctx": lax.rem(me + d, n)}

    def far_first(i):
        return n // 2 + (1 - 2 * (i % 2)) * ((i + 1) // 2)

    def sends(make):
        def body(i, carry):
            make(far_first(i)).start()
            return carry

        lax.fori_loop(0, n - 1, body, 0)

    def remote(src, dst, send, got, d):
        return pltpu.make_async_remote_copy(
            src_ref=src, dst_ref=dst, send_sem=send, recv_sem=got, device_id=peer(d), device_id_type=MESH
        )

    barrier = pltpu.get_barrier_semaphore()

    def greet(d, carry):
        pl.semaphore_signal(barrier, inc=1, device_id=peer(d), device_id_type=MESH)
        return carry

    lax.fori_loop(1, n, greet, 0)

    load_keys = pltpu.make_async_copy(keys_hbm.at[0], keys, load_sem.at[0])
    load_vals = pltpu.make_async_copy(vals_hbm.at[0], vals, load_sem.at[1])
    load_keys.start()
    load_vals.start()

    wanted = ref_ref[...] - me * pool_ref.shape[1]
    hit = lax.broadcasted_iota(jnp.int32, (pool_ref.shape[1], queries), 0) == wanted
    hit_t = jnp.where(hit, 1.0, 0.0).astype(F32).T.astype(BF16)
    q_part[...] = nn(hit_t, pool_ref[0]).astype(BF16)

    local = kept_ref[...] - me * rows
    local_col = jnp.broadcast_to(local, (128, kept)).T
    load_keys.wait()
    load_vals.wait()
    step = 512

    def pick(i, carry):
        at = pl.ds(pl.multiple_of(i * step, step), step)
        base = lax.broadcasted_iota(jnp.int32, (kept, 128), 1) + i * step
        hot = jnp.concatenate(
            [jnp.where(local_col == base + 128 * j, 1.0, 0.0).astype(BF16) for j in range(step // 128)], axis=1
        )
        vals_t[:, at] = vals[at, :].astype(F32).T.astype(BF16)
        return carry[0] + nn(hot, keys[at, :]), carry[1] + nn(hot, vals[at, :])

    zero = jnp.zeros((kept, head), F32)
    kept_keys, kept_vals = lax.fori_loop(0, rows // step, pick, (zero, zero))
    kk[0] = kept_keys.astype(BF16)
    v_t[...] = kept_vals.T

    pl.semaphore_wait(barrier, n - 1)

    for h in range(HALVES):

        def send_share(d, h=h):
            own = pl.ds(pl.multiple_of(h * half + lax.rem(me + d, n) * blk, blk), blk)
            return remote(q_part.at[own], q_recv.at[h, d], q_send.at[h], q_got.at[h], d)

        sends(send_share)
        mine = pl.ds(pl.multiple_of(h * half + me * blk, blk), blk)
        q_recv[h, 0] = q_part[mine, :]

    def ring(way, s):
        slot = s if way == 0 else lax.rem(n - s, n)
        there = s + 1 if way == 0 else n - s - 1
        return remote(
            kk.at[slot], kk.at[there], ring_send.at[way, s], ring_got.at[way, s], 1 if way == 0 else n - 1
        )

    right_steps, left_steps = n // 2, n - 1 - n // 2

    def ring_next(s):
        if s > 0:
            if s <= right_steps:
                ring(0, s - 1).wait_recv()
            if s <= left_steps:
                ring(1, s - 1).wait_recv()
        if s < right_steps:
            ring(0, s).start()
        if s < left_steps:
            ring(1, s).start()

    ring_next(0)

    for h in range(HALVES):
        if h == 1:
            ring_next(1)
        got = q_recv.at[h, pl.ds(1, n - 1)]
        pltpu.make_async_copy(got, got, q_got.at[h]).wait()
        total = q_recv[h, 0].astype(F32)
        for d in range(1, n):
            total = total + q_recv[h, d].astype(F32)
        q_blk[h] = total.astype(BF16)
        mine = pl.ds(pl.multiple_of(h * half + me * blk, blk), blk)

        def send_block(d, h=h, mine=mine):
            return remote(q_blk.at[h], q_all.at[mine], g_send.at[h], g_got.at[h], d)

        sends(send_block)
        q_all[mine, :] = q_blk[h]

    def send_vals(d):
        own = pl.ds(pl.multiple_of(lax.rem(me + d, n) * cols, cols), cols)
        return remote(v_t.at[own], v_recv.at[d], v_send, v_got, d)

    sends(send_vals)
    v_recv[0] = v_t[pl.ds(pl.multiple_of(me * cols, cols), cols), :]
    ring_next(2)
    ring_next(3)

    for h in range(HALVES):
        got = q_all.at[pl.ds(0, (n - 1) * blk)]
        pltpu.make_async_copy(got, got, g_got.at[h]).wait()
        q_half = q_all[h * half : (h + 1) * half, :]

        def score(i, top):
            at = pl.ds(pl.multiple_of(i * step, step), step)
            s = nt(keys[at, :], q_half) * scale
            s_buf[at, :] = s
            return jnp.maximum(top, jnp.max(s.reshape(step // 8, 8, half), axis=0))

        top = lax.fori_loop(0, rows // step, score, jnp.full((8, half), -jnp.inf, F32))
        top = jnp.max(top, axis=0, keepdims=True)

        def weigh(i, carry):
            at = pl.ds(pl.multiple_of(i * step, step), step)
            e = jnp.exp(s_buf[at, :] - top)
            total = carry[0] + jnp.sum(e.reshape(step // 8, 8, half), axis=0)
            return total, carry[1] + nn(vals_t[:, at], e.astype(BF16))

        total, weighted = lax.fori_loop(
            0, rows // step, weigh, (jnp.zeros((8, half), F32), jnp.zeros((head, half), F32))
        )
        total = jnp.sum(total, axis=0, keepdims=True)
        p_t[h] = weighted
        for j in range(half // 128):
            stats[h, j : j + 1, :] = top[:, j * 128 : (j + 1) * 128]
            stats[h, 2 + j : 3 + j, :] = total[:, j * 128 : (j + 1) * 128]

        def send_weighted(d, h=h):
            own = pl.ds(pl.multiple_of(lax.rem(me + d, n) * cols, cols), cols)
            return remote(p_t.at[h, own], p_recv.at[h, d], p_send.at[h], p_got.at[h], d)

        def send_stats(d, h=h):
            return remote(stats.at[h], stats_recv.at[h, d], st_send.at[h], st_got.at[h], d)

        sends(send_stats)
        sends(send_weighted)
        p_recv[h, 0] = p_t[h, pl.ds(pl.multiple_of(me * cols, cols), cols), :]
        stats_recv[h, 0] = stats[h]
        ring_next(4 + h)

    q_now = q_all[...]
    top_buf[...] = jnp.full(top_buf.shape, -jnp.inf, F32)

    def kept_scores(slot):
        s = nt(q_now, kk[slot]) * scale
        a_buf[:, pl.ds(pl.multiple_of(slot * kept, kept), kept)] = s
        best = top_buf[...]
        for j in range(kept // 128):
            best = jnp.maximum(best, s[:, j * 128 : (j + 1) * 128])
        top_buf[...] = best

    def kept_scores_body(slot, carry):
        kept_scores(slot)
        return carry

    done_right, done_left = 5, 5
    lax.fori_loop(0, done_right + 1, kept_scores_body, 0)
    lax.fori_loop(n - done_left, n, kept_scores_body, 0)
    for s in range(6, right_steps + 1):
        ring_next(s)
        kept_scores(s)
        if s <= left_steps:
            kept_scores(n - s)
    best = jnp.max(top_buf[...], axis=1, keepdims=True)
    top_buf[...] = jnp.broadcast_to(best, top_buf.shape)

    def kept_weights(i, carry):
        at = pl.ds(pl.multiple_of(i * 128, 128), 128)
        high, low = split(jnp.exp(a_buf[:, at] - top_buf[...]))
        a_high[:, at] = high
        a_low[:, at] = low
        return carry

    lax.fori_loop(0, n * kept // 128, kept_weights, 0)

    got = v_recv.at[pl.ds(1, n - 1)]
    pltpu.make_async_copy(got, got, v_got).wait()
    vals_here = jnp.concatenate([v_recv[d] for d in range(n)], axis=1)
    rows_aug = jnp.concatenate([vals_here, jnp.ones_like(vals_here)], axis=0).astype(BF16)
    fitted_now = nt(rows_aug, a_high[...]) + nt(rows_aug, a_low[...])
    inverse = 1.0 / fitted_now[cols : cols + 1, :]
    fitted_now = fitted_now[:cols, :] * inverse

    def products(i, carry):
        at = pl.ds(pl.multiple_of(i * 256, 256), 256)
        gram[:, at] = nt(a_high[...], a_low[at, :])
        return carry

    lax.fori_loop(0, queries // 256, products, 0)
    gram[...] = gram[...] + gram[...].T

    def squares(i, carry):
        at = pl.ds(pl.multiple_of(i * 256, 256), 256)
        gram[:, at] = gram[:, at] + nt(a_high[...], a_high[at, :])
        return carry

    lax.fori_loop(0, queries // 256, squares, 0)
    gram_high, gram_low = split(gram[...])

    pieces = []
    for h in range(HALVES):
        got = stats_recv.at[h, pl.ds(1, n - 1)]
        pltpu.make_async_copy(got, got, st_got.at[h]).wait()
        got = p_recv.at[h, pl.ds(1, n - 1)]
        pltpu.make_async_copy(got, got, p_got.at[h]).wait()
        for j in range(half // 128):
            tops = stats_recv[h, :, j : j + 1, :]
            totals = stats_recv[h, :, 2 + j : 3 + j, :]
            factor = jnp.exp(tops - jnp.max(tops, axis=0, keepdims=True))
            weighted = jnp.sum(factor * p_recv[h, :, :, j * 128 : (j + 1) * 128], axis=0)
            pieces.append(weighted / jnp.sum(factor * totals, axis=0))
    target = jnp.concatenate(pieces, axis=1)

    def apply(x):
        high, low = split(x * inverse)
        both = nn(jnp.concatenate([high, low], axis=0), gram_high)
        return (both[:cols] + both[cols:] + nn(high, gram_low)) * inverse

    def dots(a, b):
        return jnp.sum(a * b, axis=1, keepdims=True)

    y = target - fitted_now
    image_y = apply(y)
    norm_now = dots(y, image_y)
    u, image = y, image_y
    answer = jnp.zeros_like(y)
    for it in range(ITERS):
        curve = dots(image, image) + ridge * dots(u, image)
        alpha = norm_now / curve
        answer = answer + alpha * u
        if it == ITERS - 1:
            break
        y = y - alpha * (image + ridge * u)
        image_y = apply(y)
        norm_next = dots(y, image_y)
        beta = norm_next / norm_now
        u = y + beta * u
        image = image_y + beta * image
        norm_now = norm_next

    high, low = split(answer * inverse)
    both_ways = jnp.concatenate([high, low], axis=0)
    own_cols = pl.ds(pl.multiple_of(me * cols, cols), cols)

    def result(slot):
        at = pl.ds(pl.multiple_of(slot * kept, kept), kept)
        both = nn(both_ways, a_high[:, at])
        return v_recv[slot] + both[:cols] + both[cols:] + nn(high, a_low[:, at])

    def give(i, carry):
        d = far_first(i)
        res[d] = result(n - d)
        remote(res.at[d], fin.at[own_cols], f_send, f_got, d).start()
        return carry

    lax.fori_loop(0, n - 1, give, 0)
    fin[own_cols, :] = result(0)

    def drain(ref, sem):
        pltpu.make_async_copy(ref, ref, sem).wait()

    for h in range(HALVES):
        drain(q_recv.at[h, pl.ds(1, n - 1)], q_send.at[h])
        drain(q_all.at[pl.ds(0, (n - 1) * blk)], g_send.at[h])
        drain(p_recv.at[h, pl.ds(1, n - 1)], p_send.at[h])
        drain(stats_recv.at[h, pl.ds(1, n - 1)], st_send.at[h])
    drain(v_recv.at[pl.ds(1, n - 1)], v_send)
    for s in range(right_steps):
        ring(0, s).wait_send()
        if s < left_steps:
            ring(1, s).wait_send()
    drain(res.at[pl.ds(1, n - 1)], f_send)
    drain(res.at[pl.ds(1, n - 1)], f_got)
    out_ref[0] = fin[...].T


def local(cache_keys, cache_values, query_pool, kept_index, ref_index):
    n = lax.axis_size("ctx")
    rows, head = cache_keys.shape[1:]
    kept = kept_index.shape[1]
    queries = ref_index.shape[1]
    half = queries // HALVES
    blk = half // n
    cols = head // n
    vmem = pl.BlockSpec(memory_space=pltpu.VMEM)
    hbm = pl.BlockSpec(memory_space=pl.ANY)
    dma = pltpu.SemaphoreType.DMA
    return pl.pallas_call(
        functools.partial(kernel, n),
        out_shape=jax.ShapeDtypeStruct((1, kept, head), F32),
        in_specs=[hbm, hbm, vmem, vmem, vmem],
        out_specs=vmem,
        scratch_shapes=[
            pltpu.VMEM((rows, head), BF16),
            pltpu.VMEM((rows, head), BF16),
            pltpu.VMEM((head, rows), BF16),
            pltpu.VMEM((queries, head), BF16),
            pltpu.VMEM((HALVES, n, blk, head), BF16),
            pltpu.VMEM((HALVES, blk, head), BF16),
            pltpu.VMEM((queries, head), BF16),
            pltpu.VMEM((n, kept, head), BF16),
            pltpu.VMEM((head, kept), F32),
            pltpu.VMEM((n, cols, kept), F32),
            pltpu.VMEM((rows, half), F32),
            pltpu.VMEM((HALVES, head, half), F32),
            pltpu.VMEM((HALVES, 4, 128), F32),
            pltpu.VMEM((HALVES, n, cols, half), F32),
            pltpu.VMEM((HALVES, n, 4, 128), F32),
            pltpu.VMEM((queries, n * kept), F32),
            pltpu.VMEM((queries, 128), F32),
            pltpu.VMEM((queries, n * kept), BF16),
            pltpu.VMEM((queries, n * kept), BF16),
            pltpu.VMEM((queries, queries), F32),
            pltpu.VMEM((n, cols, kept), F32),
            pltpu.VMEM((head, kept), F32),
            dma((2,)),
            dma((HALVES,)),
            dma((HALVES,)),
            dma((HALVES,)),
            dma((HALVES,)),
            dma((2, n)),
            dma((2, n)),
            dma,
            dma,
            dma((HALVES,)),
            dma((HALVES,)),
            dma((HALVES,)),
            dma((HALVES,)),
            dma,
            dma,
        ],
        compiler_params=pltpu.CompilerParams(
            collective_id=0, has_side_effects=True, vmem_limit_bytes=56 * 1024 * 1024
        ),
    )(cache_keys, cache_values, query_pool, kept_index, ref_index)


def solution(mesh):
    placed = (
        P("rep", "ctx", None),
        P("rep", "ctx", None),
        P("rep", "ctx", None),
        P("rep", "ctx"),
        P("rep", None),
    )
    return jax.shard_map(
        local, mesh=mesh, in_specs=placed, out_specs=P("rep", "ctx", None), check_vma=False
    )
```

```python
import functools

import jax
import jax.numpy as jnp
from jax import lax
from jax.experimental import pallas as pl
from jax.experimental.pallas import tpu as pltpu
from jax.sharding import PartitionSpec as P

ITERS = 3
HALVES = 2
OWNERS = 2
NEAR = 4
F32 = jnp.float32
BF16 = jnp.bfloat16
MESH = pl.DeviceIdType.MESH


def nt(a, b):
    return lax.dot_general(a, b, (((1,), (1,)), ((), ())), preferred_element_type=F32)


def nn(a, b):
    return lax.dot_general(a, b, (((1,), (0,)), ((), ())), preferred_element_type=F32)


def split(x):
    high = x.astype(BF16)
    return high, (x - high.astype(F32)).astype(BF16)


def kernel(
    n, keys_hbm, vals_hbm, pool_ref, kept_ref, ref_ref, out_ref,
    keys, vals, vals_t, q_part, q_recv, q_blk, q_all, kk_own, kk, v_t, v_recv,
    s_buf, p_t, stats, p_near, stats_near, p_sum, stats_sum, p_recv, stats_recv, a_buf, top_buf, a_high, a_low, gram, low_sums, res, fin,
    load_sem, q_send, q_got, g_send, g_got, kept_send, kept_got, v_send, v_got,
    p_send, p_got, st_send, st_got, ps_send, ps_got, sts_send, sts_got, f_send, f_got,
):
    me = lax.axis_index("ctx")
    rows, head = keys.shape
    kept = kk.shape[1]
    queries = q_all.shape[0]
    half = queries // HALVES
    blk = half // n
    cols = head // OWNERS
    apart = n // OWNERS
    scale = 1.0 / head**0.5
    ridge = 0.3 * queries / ((kept * n) * (kept * n))

    def peer(d):
        return {"ctx": lax.rem(me + d, n)}

    core = lax.rem(lax.axis_index("rep"), 2)
    offset = core * (apart // 2)
    place = lax.rem(me - offset + n, apart)
    owner = place == 0
    seat = lax.rem(place + NEAR - 1 - 2 * core, NEAR)

    def owned(ahead):
        first = lax.rem(me - place + ahead * apart - offset + n, n) // apart * cols
        return pl.ds(pl.multiple_of(first, cols), cols)

    def to_owners(send, keep):
        for ahead in reversed(range(OWNERS)):
            if ahead > 0:
                for copy in send(ahead, ahead * apart - place + n, lax.rem(place - ahead * apart + n, n)):
                    copy.start()
            else:

                @pl.when(place > 0)
                def _():
                    for copy in send(0, n - place, place):
                        copy.start()

                @pl.when(owner)
                def _():
                    keep()

    def sent_to_owners(send):
        for ahead in range(1, OWNERS):
            for copy in send(ahead, ahead * apart - place + n, lax.rem(place - ahead * apart + n, n)):
                copy.wait_send()

        @pl.when(place > 0)
        def _():
            for copy in send(0, n - place, place):
                copy.wait_send()

    def far_first(i):
        return n // 2 + (1 - 2 * (i % 2)) * ((i + 1) // 2)

    def sends(make):
        def body(i, carry):
            make(far_first(i)).start()
            return carry

        lax.fori_loop(0, n - 1, body, 0)

    def remote(src, dst, send, got, d):
        return pltpu.make_async_remote_copy(
            src_ref=src, dst_ref=dst, send_sem=send, recv_sem=got, device_id=peer(d), device_id_type=MESH
        )

    barrier = pltpu.get_barrier_semaphore()

    def greet(d, carry):
        pl.semaphore_signal(barrier, inc=1, device_id=peer(d), device_id_type=MESH)
        return carry

    lax.fori_loop(1, n, greet, 0)

    load_keys = pltpu.make_async_copy(keys_hbm.at[0], keys, load_sem.at[0])
    load_vals = pltpu.make_async_copy(vals_hbm.at[0], vals, load_sem.at[1])
    load_keys.start()
    load_vals.start()

    wanted = ref_ref[...] - me * pool_ref.shape[1]
    hit = lax.broadcasted_iota(jnp.int32, (pool_ref.shape[1], queries), 0) == wanted
    hit_t = jnp.where(hit, 1.0, 0.0).astype(F32).T.astype(BF16)
    q_part[...] = nn(hit_t, pool_ref[0]).astype(BF16)

    local = kept_ref[...] - me * rows
    local_col = jnp.broadcast_to(local, (128, kept)).T
    step = 512

    def chosen(i):
        base = lax.broadcasted_iota(jnp.int32, (kept, 128), 1) + i * step
        return jnp.concatenate(
            [jnp.where(local_col == base + 128 * j, 1.0, 0.0).astype(BF16) for j in range(step // 128)], axis=1
        )

    load_keys.wait()

    def pick_keys(i, carry):
        return carry + nn(chosen(i), keys[pl.ds(pl.multiple_of(i * step, step), step), :])

    kk_own[...] = lax.fori_loop(0, rows // step, pick_keys, jnp.zeros((kept, head), F32)).astype(BF16)

    def send_kept(ahead, d, slot):
        return (remote(kk_own, kk.at[slot], kept_send.at[ahead], kept_got.at[slot], d),)

    def keep_kept():
        kk[0] = kk_own[...]

    def send_vals(ahead, d, slot):
        return (remote(v_t.at[owned(ahead)], v_recv.at[slot], v_send.at[ahead], v_got, d),)

    def keep_vals():
        v_recv[0] = v_t[owned(0), :]

    pl.semaphore_wait(barrier, n - 1)

    for h in range(HALVES):

        def send_share(d, h=h):
            own = pl.ds(pl.multiple_of(h * half + lax.rem(me + d, n) * blk, blk), blk)
            return remote(q_part.at[own], q_recv.at[h, d], q_send.at[h], q_got.at[h], d)

        sends(send_share)
        mine = pl.ds(pl.multiple_of(h * half + me * blk, blk), blk)
        q_recv[h, 0] = q_part[mine, :]


    load_vals.wait()

    def pick_vals(i, carry):
        at = pl.ds(pl.multiple_of(i * step, step), step)
        vals_t[:, at] = vals[at, :].astype(F32).T.astype(BF16)
        return carry + nn(chosen(i), vals[at, :])

    kept_vals = lax.fori_loop(0, rows // step, pick_vals, jnp.zeros((kept, head), F32))
    v_t[...] = kept_vals.T.astype(BF16)

    for h in range(HALVES):
        got = q_recv.at[h, pl.ds(1, n - 1)]
        pltpu.make_async_copy(got, got, q_got.at[h]).wait()
        total = q_recv[h, 0].astype(F32)
        for d in range(1, n):
            total = total + q_recv[h, d].astype(F32)
        q_blk[h] = total.astype(BF16)
        mine = pl.ds(pl.multiple_of(h * half + me * blk, blk), blk)

        def send_block(d, h=h, mine=mine):
            return remote(q_blk.at[h], q_all.at[mine], g_send.at[h], g_got.at[h], d)

        sends(send_block)
        q_all[mine, :] = q_blk[h]


    def near_target(h, d, slot):
        return (
            remote(stats.at[h], stats_near.at[h, slot], st_send.at[h], st_got.at[h, slot], d),
            remote(p_t.at[h], p_near.at[h, slot], p_send.at[h], p_got.at[h, slot], d),
        )

    for h in range(HALVES):
        got = q_all.at[pl.ds(0, (n - 1) * blk)]
        pltpu.make_async_copy(got, got, g_got.at[h]).wait()
        if h == 0:
            to_owners(send_kept, keep_kept)
        if h == 1:
            to_owners(send_vals, keep_vals)
        q_half = q_all[h * half : (h + 1) * half, :]

        def score(i, top):
            at = pl.ds(pl.multiple_of(i * step, step), step)
            s = nt(keys[at, :], q_half) * scale
            s_buf[at, :] = s
            return jnp.maximum(top, jnp.max(s.reshape(step // 8, 8, half), axis=0))

        top = lax.fori_loop(0, rows // step, score, jnp.full((8, half), -jnp.inf, F32))
        top = jnp.max(top, axis=0, keepdims=True)

        def weigh(i, carry):
            at = pl.ds(pl.multiple_of(i * step, step), step)
            e = jnp.exp(s_buf[at, :] - top)
            total = carry[0] + jnp.sum(e.reshape(step // 8, 8, half), axis=0)
            return total, carry[1] + nn(vals_t[:, at], e.astype(BF16))

        total, weighted = lax.fori_loop(
            0, rows // step, weigh, (jnp.zeros((8, half), F32), jnp.zeros((head, half), F32))
        )
        total = jnp.sum(total, axis=0, keepdims=True)
        p_t[h] = weighted
        for j in range(half // 128):
            stats[h, j : j + 1, :] = top[:, j * 128 : (j + 1) * 128]
            stats[h, 2 + j : 3 + j, :] = total[:, j * 128 : (j + 1) * 128]

        for where, d, slot in ((1, n - 1, 1), (3, 1, 2), (2, n - 2 if h == 0 else 2, 3)):

            @pl.when(seat == where)
            def _(h=h, d=d, slot=slot):
                for copy in near_target(h, d, slot):
                    copy.start()

    def columns_at(d):
        return pl.ds(pl.multiple_of(lax.rem(me + d - offset + 2 * n, n) // apart * cols, cols), cols)

    below, above = (n - place, place // NEAR), (apart - place, place // NEAR + 2)

    def far_target(h, route):
        d, slot = route
        return (
            remote(stats_sum.at[h], stats_recv.at[h, slot], sts_send.at[h, slot], sts_got.at[h, slot], d),
            remote(p_sum.at[h, columns_at(d)], p_recv.at[h, slot], ps_send.at[h, slot], ps_got.at[h, slot], d),
        )

    def merge_near(h):
        for slot in (1, 2, 3):
            for copy in near_target(h, 1, slot):
                copy.wait_recv()
        for j in range(half // 128):
            lanes = slice(j * 128, (j + 1) * 128)
            tops = [stats[h, j : j + 1, :]] + [stats_near[h, slot, j : j + 1, :] for slot in (1, 2, 3)]
            best = functools.reduce(jnp.maximum, tops)
            factors = [jnp.exp(top - best) for top in tops]
            total = factors[0] * stats[h, 2 + j : 3 + j, :]
            weighted = factors[0] * p_t[h, :, lanes]
            for slot in (1, 2, 3):
                total = total + factors[slot] * stats_near[h, slot, 2 + j : 3 + j, :]
                weighted = weighted + factors[slot] * p_near[h, slot, :, lanes]
            stats_sum[h, j : j + 1, :] = best
            stats_sum[h, 2 + j : 3 + j, :] = total
            p_sum[h, :, lanes] = weighted

    @pl.when(seat == 0)
    def _():
        for h in range(HALVES):
            merge_near(h)
            for route in (below, above):
                for copy in far_target(h, route):
                    copy.start()

    @pl.when(owner)
    def _():
        q_now = q_all[...]
        top_buf[...] = jnp.full(top_buf.shape, -jnp.inf, F32)

        def kept_scores(slot):
            s = nt(q_now, kk[slot]) * scale
            a_buf[:, pl.ds(pl.multiple_of(slot * kept, kept), kept)] = s
            best = top_buf[...]
            for j in range(kept // 128):
                best = jnp.maximum(best, s[:, j * 128 : (j + 1) * 128])
            top_buf[...] = best

        def kept_scores_body(slot, carry):
            kept_scores(slot)
            return carry

        kept_scores(0)

        def arrived(i, carry):
            slot = i + 1 + (i + 1) // 8 * (n + 5 - 2 * i)
            pltpu.make_async_copy(kk.at[slot], kk.at[slot], kept_got.at[slot]).wait()
            kept_scores(slot)
            return carry

        lax.fori_loop(0, n - 1, arrived, 0)
        best = jnp.max(top_buf[...], axis=1, keepdims=True)
        top_buf[...] = jnp.broadcast_to(best, top_buf.shape)

        def kept_weights(i, carry):
            at = pl.ds(pl.multiple_of(i * 128, 128), 128)
            high, low = split(jnp.exp(a_buf[:, at] - top_buf[...]))
            a_high[:queries, at] = high
            a_low[:, at] = low + low
            return carry

        lax.fori_loop(0, n * kept // 128, kept_weights, 0)

        got = v_recv.at[pl.ds(1, n - 1)]
        pltpu.make_async_copy(got, got, v_got).wait()
        for d in range(n):
            a_high[queries : queries + cols, d * kept : (d + 1) * kept] = v_recv[d]
        a_high[queries + cols :, :] = jnp.ones((16, n * kept), BF16)
        def products(i, carry):
            at = pl.ds(pl.multiple_of(i * 256, 256), 256)
            gram[:, at] = nt(a_high[...], a_high[at, :])
            low_sums[:, at] = nt(a_high[...], a_low[at, :])
            return carry

        lax.fori_loop(0, queries // 256, products, 0)
        sums = gram[queries:, :] + 0.5 * low_sums[queries:, :]
        inverse = 1.0 / sums[cols : cols + 1, :]
        fitted_now = sums[:cols, :] * inverse
        once = gram[:queries, :] + low_sums[:queries, :]
        gram_high, gram_low = split(0.5 * (once + once.T))

        pieces = []
        for h in range(HALVES):
            for slot in range(4):
                for copy in far_target(h, (NEAR, slot)):
                    copy.wait_recv()
            for j in range(half // 128):
                tops = stats_recv[h, :, j : j + 1, :]
                totals = stats_recv[h, :, 2 + j : 3 + j, :]
                factor = jnp.exp(tops - jnp.max(tops, axis=0, keepdims=True))
                weighted = jnp.sum(factor * p_recv[h, :, :, j * 128 : (j + 1) * 128], axis=0)
                pieces.append(weighted / jnp.sum(factor * totals, axis=0))
        target = jnp.concatenate(pieces, axis=1)

        def apply(x):
            high, low = split(x * inverse)
            both = nn(jnp.concatenate([high, low], axis=0), gram_high)
            return (both[:cols] + both[cols:] + nn(high, gram_low)) * inverse

        def dots(a, b):
            return jnp.sum(a * b, axis=1, keepdims=True)

        y = target - fitted_now
        image_y = apply(y)
        norm_now = dots(y, image_y)
        u, image = y, image_y
        answer = jnp.zeros_like(y)
        for it in range(ITERS):
            curve = dots(image, image) + ridge * dots(u, image)
            alpha = norm_now / curve
            answer = answer + alpha * u
            if it == ITERS - 1:
                break
            y = y - alpha * (image + ridge * u)
            image_y = apply(y)
            norm_next = dots(y, image_y)
            beta = norm_next / norm_now
            u = y + beta * u
            image = image_y + beta * image
            norm_now = norm_next

        high, low = split(answer * inverse)
        both_ways = jnp.concatenate([high, low], axis=0)

        def result(slot):
            at = pl.ds(pl.multiple_of(slot * kept, kept), kept)
            both = nn(both_ways, a_high[:queries, at])
            return v_recv[slot].astype(F32) + both[:cols] + both[cols:] + 0.5 * nn(high, a_low[:, at])

        def give(i, carry):
            d = far_first(i)
            res[d] = result(d)
            remote(res.at[d], fin.at[owned(0)], f_send, f_got, d).start()
            return carry

        lax.fori_loop(0, n - 1, give, 0)
        fin[owned(0), :] = result(0)

    def drain(ref, sem):
        pltpu.make_async_copy(ref, ref, sem).wait()

    for h in range(HALVES):
        drain(q_recv.at[h, pl.ds(1, n - 1)], q_send.at[h])
        drain(q_all.at[pl.ds(0, (n - 1) * blk)], g_send.at[h])
    sent_to_owners(send_vals)
    sent_to_owners(send_kept)

    @pl.when(owner)
    def _():
        drain(res.at[pl.ds(1, n - 1)], f_send)
        drain(fin.at[pl.ds(0, head - cols)], f_got)

    @pl.when(seat == 0)
    def _():
        for h in range(HALVES):
            for route in (below, above):
                for copy in far_target(h, route):
                    copy.wait_send()

    @pl.when(seat > 0)
    def _():
        for h in range(HALVES):
            for copy in near_target(h, 1, 1):
                copy.wait_send()

    @pl.when(place > 0)
    def _():
        drain(fin, f_got)

    out_ref[0] = fin[...].T


def local(cache_keys, cache_values, query_pool, kept_index, ref_index):
    n = lax.axis_size("ctx")
    rows, head = cache_keys.shape[1:]
    kept = kept_index.shape[1]
    queries = ref_index.shape[1]
    half = queries // HALVES
    blk = half // n
    cols = head // OWNERS
    vmem = pl.BlockSpec(memory_space=pltpu.VMEM)
    hbm = pl.BlockSpec(memory_space=pl.ANY)
    dma = pltpu.SemaphoreType.DMA
    return pl.pallas_call(
        functools.partial(kernel, n),
        out_shape=jax.ShapeDtypeStruct((1, kept, head), F32),
        in_specs=[hbm, hbm, vmem, vmem, vmem],
        out_specs=vmem,
        scratch_shapes=[
            pltpu.VMEM((rows, head), BF16),
            pltpu.VMEM((rows, head), BF16),
            pltpu.VMEM((head, rows), BF16),
            pltpu.VMEM((queries, head), BF16),
            pltpu.VMEM((HALVES, n, blk, head), BF16),
            pltpu.VMEM((HALVES, blk, head), BF16),
            pltpu.VMEM((queries, head), BF16),
            pltpu.VMEM((kept, head), BF16),
            pltpu.VMEM((n, kept, head), BF16),
            pltpu.VMEM((head, kept), BF16),
            pltpu.VMEM((n, cols, kept), BF16),
            pltpu.VMEM((rows, half), F32),
            pltpu.VMEM((HALVES, head, half), F32),
            pltpu.VMEM((HALVES, 4, 128), F32),
            pltpu.VMEM((HALVES, 4, head, half), F32),
            pltpu.VMEM((HALVES, 4, 4, 128), F32),
            pltpu.VMEM((HALVES, head, half), F32),
            pltpu.VMEM((HALVES, 4, 128), F32),
            pltpu.VMEM((HALVES, 4, cols, half), F32),
            pltpu.VMEM((HALVES, 4, 4, 128), F32),
            pltpu.VMEM((queries, n * kept), F32),
            pltpu.VMEM((queries, 128), F32),
            pltpu.VMEM((queries + cols + 16, n * kept), BF16),
            pltpu.VMEM((queries, n * kept), BF16),
            pltpu.VMEM((queries + cols + 16, queries), F32),
            pltpu.VMEM((queries + cols + 16, queries), F32),
            pltpu.VMEM((n, cols, kept), F32),
            pltpu.VMEM((head, kept), F32),
            dma((2,)),
            dma((HALVES,)),
            dma((HALVES,)),
            dma((HALVES,)),
            dma((HALVES,)),
            dma((OWNERS,)),
            dma((n,)),
            dma((OWNERS,)),
            dma,
            dma((HALVES,)),
            dma((HALVES, 4)),
            dma((HALVES,)),
            dma((HALVES, 4)),
            dma((HALVES, 4)),
            dma((HALVES, 4)),
            dma((HALVES, 4)),
            dma((HALVES, 4)),
            dma,
            dma,
        ],
        compiler_params=pltpu.CompilerParams(
            collective_id=0, has_side_effects=True, vmem_limit_bytes=56 * 1024 * 1024
        ),
    )(cache_keys, cache_values, query_pool, kept_index, ref_index)


def solution(mesh):
    placed = (
        P("rep", "ctx", None),
        P("rep", "ctx", None),
        P("rep", "ctx", None),
        P("rep", "ctx"),
        P("rep", None),
    )
    return jax.shard_map(
        local, mesh=mesh, in_specs=placed, out_specs=P("rep", "ctx", None), check_vma=False
    )
```

```python
import functools

import jax
import jax.numpy as jnp
from jax import lax
from jax.experimental import pallas as pl
from jax.experimental.pallas import tpu as pltpu
from jax.sharding import PartitionSpec as P

ITERS = 3
HALVES = 2
OWNERS = 2
NEAR = 4
F32 = jnp.float32
BF16 = jnp.bfloat16
MESH = pl.DeviceIdType.MESH


def nt(a, b):
    return lax.dot_general(a, b, (((1,), (1,)), ((), ())), preferred_element_type=F32)


def nn(a, b):
    return lax.dot_general(a, b, (((1,), (0,)), ((), ())), preferred_element_type=F32)


def split(x):
    high = x.astype(BF16)
    return high, (x - high.astype(F32)).astype(BF16)


def kernel(
    n, keys_hbm, vals_hbm, pool_hbm, kept_hbm, ref_hbm, out_ref,
    pool_ref, kept_ref, ref_ref,
    keys, vals, vals_t, q_part, q_recv, q_blk, q_all, kk_own, kk, v_t, v_recv,
    s_buf, p_t, stats, p_near, stats_near, p_sum, stats_sum, p_recv, stats_recv, a_buf, top_buf, a_both, rows_v, gram, res, fin, units, fin_units, turned, vals_own,
    load_sem, q_send, q_got, g_send, g_got, kept_send, kept_got, v_send, v_got,
    p_send, p_got, st_send, st_got, ps_send, ps_got, sts_send, sts_got, f_send, f_got, u_send, u_got,
):
    me = lax.axis_index("ctx")
    rows, head = keys.shape
    kept = kk.shape[1]
    queries = q_all.shape[0]
    half = queries // HALVES
    blk = half // n
    cols = head // OWNERS
    apart = n // OWNERS
    scale = 1.0 / head**0.5
    ridge = 0.3 * queries / ((kept * n) * (kept * n))

    def peer(d):
        return {"ctx": lax.rem(me + d, n)}

    core = lax.rem(lax.axis_index("rep"), 2)
    offset = core * (apart // 2)
    place = lax.rem(me - offset + n, apart)
    owner = place == 0
    seat = lax.rem(place + NEAR - 1 - 2 * core, NEAR)

    column_block = lax.rem(me - place - offset + n, n) // apart

    def owned(ahead):
        first = lax.rem(me - place + ahead * apart - offset + n, n) // apart * cols
        return pl.ds(pl.multiple_of(first, cols), cols)

    def to_owners(send, keep):
        for ahead in reversed(range(OWNERS)):
            if ahead > 0:
                for copy in send(ahead, ahead * apart - place + n, lax.rem(place - ahead * apart + n, n)):
                    copy.start()
            else:

                @pl.when(place > 0)
                def _():
                    for copy in send(0, n - place, place):
                        copy.start()

                @pl.when(owner)
                def _():
                    keep()

    def sent_to_owners(send):
        for ahead in range(1, OWNERS):
            for copy in send(ahead, ahead * apart - place + n, lax.rem(place - ahead * apart + n, n)):
                copy.wait_send()

        @pl.when(place > 0)
        def _():
            for copy in send(0, n - place, place):
                copy.wait_send()

    def far_first(i):
        return n // 2 + (1 - 2 * (i % 2)) * ((i + 1) // 2)

    def sends(make):
        def body(i, carry):
            make(far_first(i)).start()
            return carry

        lax.fori_loop(0, n - 1, body, 0)

    def remote(src, dst, send, got, d):
        return pltpu.make_async_remote_copy(
            src_ref=src, dst_ref=dst, send_sem=send, recv_sem=got, device_id=peer(d), device_id_type=MESH
        )

    barrier = pltpu.get_barrier_semaphore()

    def greet(d, carry):
        pl.semaphore_signal(barrier, inc=1, device_id=peer(d), device_id_type=MESH)
        return carry

    lax.fori_loop(1, n, greet, 0)

    loads = [
        pltpu.make_async_copy(src, dst, load_sem.at[2 + i])
        for i, (src, dst) in enumerate(((ref_hbm, ref_ref), (pool_hbm, pool_ref), (kept_hbm, kept_ref)))
    ]
    for load in loads:
        load.start()
    load_keys = pltpu.make_async_copy(keys_hbm.at[0], keys, load_sem.at[0])
    load_vals = pltpu.make_async_copy(vals_hbm.at[0], vals, load_sem.at[1])
    load_keys.start()
    load_vals.start()

    for load in loads:
        load.wait()
    wanted = ref_ref[...] - me * pool_ref.shape[1]
    hit = lax.broadcasted_iota(jnp.int32, (pool_ref.shape[1], queries), 0) == wanted
    hit_t = jnp.where(hit, 1.0, 0.0).astype(F32).T.astype(BF16)
    q_part[...] = nn(hit_t, pool_ref[0]).astype(BF16)

    local = kept_ref[...] - me * rows
    local_col = jnp.broadcast_to(local, (128, kept)).T
    step = 512

    def chosen(i):
        base = lax.broadcasted_iota(jnp.int32, (kept, 128), 1) + i * step
        return jnp.concatenate(
            [jnp.where(local_col == base + 128 * j, 1.0, 0.0).astype(BF16) for j in range(step // 128)], axis=1
        )

    load_keys.wait()

    def pick_keys(i, carry):
        return carry + nn(chosen(i), keys[pl.ds(pl.multiple_of(i * step, step), step), :])

    kk_own[...] = lax.fori_loop(0, rows // step, pick_keys, jnp.zeros((kept, head), F32)).astype(BF16)

    def send_kept(ahead, d, slot):
        return (remote(kk_own, kk.at[slot], kept_send.at[ahead], kept_got.at[slot], d),)

    def keep_kept():
        kk[0] = kk_own[...]

    def send_vals(ahead, d, slot):
        return (remote(v_t.at[owned(ahead)], v_recv.at[slot], v_send.at[ahead], v_got, d),)

    def keep_vals():
        v_recv[0] = v_t[owned(0), :]

    pl.semaphore_wait(barrier, n - 1)

    for h in range(HALVES):

        def send_share(d, h=h):
            own = pl.ds(pl.multiple_of(h * half + lax.rem(me + d, n) * blk, blk), blk)
            return remote(q_part.at[own], q_recv.at[h, d], q_send.at[h], q_got.at[h], d)

        sends(send_share)
        mine = pl.ds(pl.multiple_of(h * half + me * blk, blk), blk)
        q_recv[h, 0] = q_part[mine, :]


    load_vals.wait()

    def pick_vals(i, carry):
        at = pl.ds(pl.multiple_of(i * step, step), step)
        vals_t[:, at] = vals[at, :].astype(F32).T.astype(BF16)
        return carry + nn(chosen(i), vals[at, :])

    kept_vals = lax.fori_loop(0, rows // step, pick_vals, jnp.zeros((kept, head), F32))
    vals_own[...] = kept_vals
    v_t[...] = kept_vals.T.astype(BF16)

    for h in range(HALVES):
        got = q_recv.at[h, pl.ds(1, n - 1)]
        pltpu.make_async_copy(got, got, q_got.at[h]).wait()
        total = q_recv[h, 0].astype(F32)
        for d in range(1, n):
            total = total + q_recv[h, d].astype(F32)
        q_blk[h] = total.astype(BF16)
        mine = pl.ds(pl.multiple_of(h * half + me * blk, blk), blk)

        def send_block(d, h=h, mine=mine):
            return remote(q_blk.at[h], q_all.at[mine], g_send.at[h], g_got.at[h], d)

        sends(send_block)
        q_all[mine, :] = q_blk[h]


    @pl.when(core == 0)
    def _():
        to_owners(send_kept, keep_kept)


    def near_target(h, d, slot):
        return (
            remote(stats.at[h], stats_near.at[h, slot], st_send.at[h], st_got.at[h, slot], d),
            remote(p_t.at[h], p_near.at[h, slot], p_send.at[h], p_got.at[h, slot], d),
        )

    span = min(rows, 2048)

    def attention(h, carry):
        got = q_all.at[pl.ds(0, (n - 1) * blk)]
        pltpu.make_async_copy(got, got, g_got.at[h]).wait()

        @pl.when((h == 0) & (core == 1))
        def _():
            to_owners(send_kept, keep_kept)

        q_turned = q_all[pl.ds(pl.multiple_of(h * half, half), half), :].astype(F32).T.astype(BF16)

        def score(i, top):
            at = pl.ds(pl.multiple_of(i * span, span), span)
            s = nn(keys[at, :], q_turned) * scale
            s_buf[at, :] = s
            return jnp.maximum(top, jnp.max(s.reshape(span // 8, 8, half), axis=0))

        top = lax.fori_loop(0, rows // span, score, jnp.full((8, half), -jnp.inf, F32))
        top = jnp.max(top, axis=0, keepdims=True)

        def weigh(i, carry):
            at = pl.ds(pl.multiple_of(i * span, span), span)
            e = jnp.exp(s_buf[at, :] - top)
            total = carry[0] + jnp.sum(e.reshape(span // 8, 8, half), axis=0)
            return total, carry[1] + nn(vals_t[:, at], e.astype(BF16))

        total, weighted = lax.fori_loop(
            0, rows // span, weigh, (jnp.zeros((8, half), F32), jnp.zeros((head, half), F32))
        )
        total = jnp.sum(total, axis=0, keepdims=True)
        p_t[h] = weighted
        lanes = [slice(j * 128, (j + 1) * 128) for j in range(half // 128)]
        stats[h] = jnp.concatenate([top[:, at] for at in lanes] + [total[:, at] for at in lanes], axis=0)
        for where, d, slot in ((1, n - 1, 1), (3, 1, 2), (2, n - 2 + 4 * h, 3)):

            @pl.when(seat == where)
            def _(d=d, slot=slot):
                for copy in near_target(h, d, slot):
                    copy.start()

        return carry

    lax.fori_loop(0, HALVES, attention, 0)
    to_owners(send_vals, keep_vals)

    def columns_at(d):
        return pl.ds(pl.multiple_of(lax.rem(me + d - offset + 2 * n, n) // apart * cols, cols), cols)

    below, above = (n - place, place // NEAR), (apart - place, place // NEAR + 2)

    def far_target(h, route):
        d, slot = route
        return (
            remote(stats_sum.at[h], stats_recv.at[h, slot], sts_send.at[h, slot], sts_got.at[h, slot], d),
            remote(p_sum.at[h, columns_at(d)], p_recv.at[h, slot], ps_send.at[h, slot], ps_got.at[h, slot], d),
        )

    def merge_near(h):
        for slot in (1, 2, 3):
            for copy in near_target(h, 1, slot):
                copy.wait_recv()
        for j in range(half // 128):
            lanes = slice(j * 128, (j + 1) * 128)
            tops = [stats[h, j : j + 1, :]] + [stats_near[h, slot, j : j + 1, :] for slot in (1, 2, 3)]
            best = functools.reduce(jnp.maximum, tops)
            factors = [jnp.exp(top - best) for top in tops]
            total = factors[0] * stats[h, 2 + j : 3 + j, :]
            weighted = factors[0] * p_t[h, :, lanes]
            for slot in (1, 2, 3):
                total = total + factors[slot] * stats_near[h, slot, 2 + j : 3 + j, :]
                weighted = weighted + factors[slot] * p_near[h, slot, :, lanes]
            stats_sum[h, j : j + 1, :] = best
            stats_sum[h, 2 + j : 3 + j, :] = total
            p_sum[h, :, lanes] = weighted

    @pl.when(seat == 0)
    def _():
        for h in range(HALVES):
            merge_near(h)
            for route in (below, above):
                for copy in far_target(h, route):
                    copy.start()

    @pl.when(owner)
    def _():
        q_now = q_all[...]
        top_buf[...] = jnp.full(top_buf.shape, -jnp.inf, F32)

        def kept_scores(first, count):
            wide = pl.ds(pl.multiple_of(first * kept, kept), count * kept)
            s = nt(q_now, kk[pl.ds(first, count)].reshape(count * kept, head)) * scale
            a_buf[:, wide] = s
            best = top_buf[...]
            for j in range(count * kept // 128):
                best = jnp.maximum(best, s[:, j * 128 : (j + 1) * 128])
            top_buf[...] = best

        def arrived(i, carry):
            first = i // 2 * NEAR + i % 2 * (n - NEAR - i // 2 * 2 * NEAR)
            for j in range(NEAR):

                @pl.when(first + j > 0)
                def _(j=j):
                    slot = kk.at[first + j]
                    pltpu.make_async_copy(slot, slot, kept_got.at[first + j]).wait()

            kept_scores(first, NEAR)
            return carry

        lax.fori_loop(0, n // NEAR, arrived, 0)
        best = jnp.max(top_buf[...], axis=1, keepdims=True)
        top_buf[...] = jnp.broadcast_to(best, top_buf.shape)

        def kept_weights(i, carry):
            at = pl.ds(pl.multiple_of(i * 1024, 1024), 1024)
            for r in range(0, queries, 16):
                some = slice(r, r + 16)
                top = jnp.concatenate([top_buf[some, :]] * 8, axis=1)
                high, low = split(jnp.exp(a_buf[some, at] - top))
                a_both[0, some, at] = high
                a_both[1, some, at] = low + low
            return carry

        lax.fori_loop(0, n * kept // 1024, kept_weights, 0)

        def products(i, carry):
            which = i // (queries // 256)
            at = pl.ds(pl.multiple_of(i % (queries // 256) * 256, 256), 256)
            gram[which, :, at] = nt(a_both[0], a_both[which, at, :])
            return carry

        lax.fori_loop(0, 2 * (queries // 256), products, 0)
        once = gram[0] + gram[1]
        gram_high, gram_low = split(0.5 * (once + once.T))

        got = v_recv.at[pl.ds(1, n - 1)]
        pltpu.make_async_copy(got, got, v_got).wait()
        for d in range(n):
            rows_v[:cols, d * kept : (d + 1) * kept] = v_recv[d]
        rows_v[cols:, :] = jnp.ones((16, n * kept), BF16)
        rows_aug = rows_v[...]
        sums = nt(rows_aug, a_both[0]) + 0.5 * nt(rows_aug, a_both[1])
        inverse = 1.0 / sums[cols : cols + 1, :]
        fitted_now = sums[:cols, :] * inverse

        pieces = []
        for h in range(HALVES):
            for slot in range(4):
                for copy in far_target(h, (NEAR, slot)):
                    copy.wait_recv()
            for j in range(half // 128):
                tops = stats_recv[h, :, j : j + 1, :]
                totals = stats_recv[h, :, 2 + j : 3 + j, :]
                factor = jnp.exp(tops - jnp.max(tops, axis=0, keepdims=True))
                weighted = jnp.sum(factor * p_recv[h, :, :, j * 128 : (j + 1) * 128], axis=0)
                pieces.append(weighted / jnp.sum(factor * totals, axis=0))
        target = jnp.concatenate(pieces, axis=1)

        def apply(x):
            high, low = split(x * inverse)
            both = nn(jnp.concatenate([high, low], axis=0), gram_high)
            return (both[:cols] + both[cols:] + nn(high, gram_low)) * inverse

        def dots(a, b):
            return jnp.sum(a * b, axis=1, keepdims=True)

        y = target - fitted_now
        image_y = apply(y)
        norm_now = dots(y, image_y)
        u, image = y, image_y
        answer = jnp.zeros_like(y)
        for it in range(ITERS):
            curve = dots(image, image) + ridge * dots(u, image)
            alpha = norm_now / curve
            answer = answer + alpha * u
            if it == ITERS - 1:
                break
            y = y - alpha * (image + ridge * u)
            image_y = apply(y)
            norm_next = dots(y, image_y)
            beta = norm_next / norm_now
            u = y + beta * u
            image = image_y + beta * image
            norm_now = norm_next

        high, low = split(answer * inverse)
        both_ways = jnp.concatenate([high, low], axis=0)

        def give(first):
            at = pl.ds(pl.multiple_of(first * kept, 2 * kept), 2 * kept)
            both = nn(both_ways, a_both[0, :queries, at])
            change = both[:cols] + both[cols:] + 0.5 * nn(high, a_both[1, :queries, at])
            largest = jnp.max(jnp.abs(change), axis=0, keepdims=True)
            factor = jnp.where(largest > 1e-30, 32767.0 / jnp.maximum(largest, 1e-30), 0.0)
            codes = jnp.round(change * factor).astype(jnp.int32).astype(jnp.int16)
            unit = largest * (1.0 / 32767.0)
            for j in range(2):
                d = first + j
                res[d] = codes[:, j * kept : (j + 1) * kept]
                units[d] = jnp.concatenate(
                    [unit[:, j * kept + k * 128 : j * kept + (k + 1) * 128] for k in range(kept // 128)], axis=0
                )

                @pl.when(d > 0)
                def _(d=d):
                    remote(res.at[d], fin.at[owned(0)], f_send, f_got, d).start()
                    remote(units.at[d], fin_units.at[column_block], u_send, u_got, d).start()

        def give_pairs(i, carry):
            give(n // 2 + 2 * i)
            give(n // 2 - 2 - 2 * i)
            return carry

        lax.fori_loop(0, n // 4, give_pairs, 0)
        fin[owned(0), :] = res[0]
        fin_units[column_block] = units[0]

    def drain(ref, sem):
        pltpu.make_async_copy(ref, ref, sem).wait()

    for h in range(HALVES):
        drain(q_recv.at[h, pl.ds(1, n - 1)], q_send.at[h])
        drain(q_all.at[pl.ds(0, (n - 1) * blk)], g_send.at[h])
    sent_to_owners(send_vals)
    sent_to_owners(send_kept)

    @pl.when(owner)
    def _():
        drain(res.at[pl.ds(1, n - 1)], f_send)
        drain(units.at[pl.ds(1, n - 1)], u_send)
        drain(fin.at[pl.ds(0, head - cols)], f_got)
        drain(fin_units.at[pl.ds(0, OWNERS - 1)], u_got)

    @pl.when(seat == 0)
    def _():
        for h in range(HALVES):
            for route in (below, above):
                for copy in far_target(h, route):
                    copy.wait_send()

    @pl.when(seat > 0)
    def _():
        for h in range(HALVES):
            for copy in near_target(h, 1, 1):
                copy.wait_send()

    @pl.when(place > 0)
    def _():
        drain(fin, f_got)
        drain(fin_units, u_got)

    for j in range(OWNERS):
        at = slice(j * cols, (j + 1) * cols)
        unit = jnp.concatenate([fin_units[j, k : k + 1, :] for k in range(kept // 128)], axis=1)
        turned[at, :] = fin[at, :].astype(jnp.int32).astype(F32) * unit
    out_ref[0] = vals_own[...] + turned[...].T


def local(cache_keys, cache_values, query_pool, kept_index, ref_index):
    n = lax.axis_size("ctx")
    rows, head = cache_keys.shape[1:]
    kept = kept_index.shape[1]
    pool = query_pool.shape[1]
    queries = ref_index.shape[1]
    half = queries // HALVES
    blk = half // n
    cols = head // OWNERS
    vmem = pl.BlockSpec(memory_space=pltpu.VMEM)
    hbm = pl.BlockSpec(memory_space=pl.ANY)
    dma = pltpu.SemaphoreType.DMA
    return pl.pallas_call(
        functools.partial(kernel, n),
        out_shape=jax.ShapeDtypeStruct((1, kept, head), F32),
        in_specs=[hbm] * 5,
        out_specs=vmem,
        scratch_shapes=[
            pltpu.VMEM((1, pool, head), BF16),
            pltpu.VMEM((1, kept), jnp.int32),
            pltpu.VMEM((1, queries), jnp.int32),
            pltpu.VMEM((rows, head), BF16),
            pltpu.VMEM((rows, head), BF16),
            pltpu.VMEM((head, rows), BF16),
            pltpu.VMEM((queries, head), BF16),
            pltpu.VMEM((HALVES, n, blk, head), BF16),
            pltpu.VMEM((HALVES, blk, head), BF16),
            pltpu.VMEM((queries, head), BF16),
            pltpu.VMEM((kept, head), BF16),
            pltpu.VMEM((n, kept, head), BF16),
            pltpu.VMEM((head, kept), BF16),
            pltpu.VMEM((n, cols, kept), BF16),
            pltpu.VMEM((rows, half), F32),
            pltpu.VMEM((HALVES, head, half), F32),
            pltpu.VMEM((HALVES, 4, 128), F32),
            pltpu.VMEM((HALVES, 4, head, half), F32),
            pltpu.VMEM((HALVES, 4, 4, 128), F32),
            pltpu.VMEM((HALVES, head, half), F32),
            pltpu.VMEM((HALVES, 4, 128), F32),
            pltpu.VMEM((HALVES, 4, cols, half), F32),
            pltpu.VMEM((HALVES, 4, 4, 128), F32),
            pltpu.VMEM((queries, n * kept), F32),
            pltpu.VMEM((queries, 128), F32),
            pltpu.VMEM((2, queries, n * kept), BF16),
            pltpu.VMEM((cols + 16, n * kept), BF16),
            pltpu.VMEM((2, queries, queries), F32),
            pltpu.VMEM((n, cols, kept), jnp.int16),
            pltpu.VMEM((head, kept), jnp.int16),
            pltpu.VMEM((n, kept // 128, 128), F32),
            pltpu.VMEM((OWNERS, kept // 128, 128), F32),
            pltpu.VMEM((head, kept), F32),
            pltpu.VMEM((kept, head), F32),
            dma((5,)),
            dma((HALVES,)),
            dma((HALVES,)),
            dma((HALVES,)),
            dma((HALVES,)),
            dma((OWNERS,)),
            dma((n,)),
            dma((OWNERS,)),
            dma,
            dma((HALVES,)),
            dma((HALVES, 4)),
            dma((HALVES,)),
            dma((HALVES, 4)),
            dma((HALVES, 4)),
            dma((HALVES, 4)),
            dma((HALVES, 4)),
            dma((HALVES, 4)),
            dma,
            dma,
            dma,
            dma,
        ],
        compiler_params=pltpu.CompilerParams(
            collective_id=0, has_side_effects=True, vmem_limit_bytes=56 * 1024 * 1024
        ),
    )(cache_keys, cache_values, query_pool, kept_index, ref_index)


def solution(mesh):
    placed = (
        P("rep", "ctx", None),
        P("rep", "ctx", None),
        P("rep", "ctx", None),
        P("rep", "ctx"),
        P("rep", None),
    )
    return jax.shard_map(
        local, mesh=mesh, in_specs=placed, out_specs=P("rep", "ctx", None), check_vma=False
    )
```

```python
import functools

import jax
import jax.numpy as jnp
from jax import lax
from jax.experimental import pallas as pl
from jax.experimental.pallas import tpu as pltpu
from jax.sharding import PartitionSpec as P

ITERS = 3
HALVES = 2
OWNERS = 2
NEAR = 4
F32 = jnp.float32
BF16 = jnp.bfloat16
MESH = pl.DeviceIdType.MESH


def nt(a, b):
    return lax.dot_general(a, b, (((1,), (1,)), ((), ())), preferred_element_type=F32)


def nn(a, b):
    return lax.dot_general(a, b, (((1,), (0,)), ((), ())), preferred_element_type=F32)


def split(x):
    high = x.astype(BF16)
    return high, (x - high.astype(F32)).astype(BF16)


def kernel(
    n, keys_hbm, vals_hbm, pool_hbm, kept_hbm, ref_hbm, out_ref,
    pool_ref, kept_ref, ref_ref,
    keys, vals, vals_t, q_part, q_recv, q_blk, q_all, kk_own, kk, v_t, v_recv,
    s_buf, p_t, stats, p_near, stats_near, p_sum, stats_sum, p_recv, stats_recv, a_buf, top_buf, a_both, gram, res, fin, units, fin_units, turned, vals_own,
    load_sem, q_send, q_got, g_send, g_got, kept_send, kept_got, v_send, v_got,
    p_send, p_got, st_send, st_got, ps_send, ps_got, sts_send, sts_got, f_send, f_got, u_send, u_got,
):
    me = lax.axis_index("ctx")
    rows, head = keys.shape
    kept = kk.shape[1]
    queries = q_all.shape[0]
    half = queries // HALVES
    blk = half // n
    cols = head // OWNERS
    apart = n // OWNERS
    scale = 1.0 / head**0.5
    ridge = 0.3 * queries / ((kept * n) * (kept * n))

    def peer(d):
        return {"ctx": lax.rem(me + d, n)}

    core = lax.rem(lax.axis_index("rep"), 2)
    offset = core * (apart // 2)
    place = lax.rem(me - offset + n, apart)
    owner = place == 0
    seat = lax.rem(place + NEAR - 1 - 2 * core, NEAR)

    column_block = lax.rem(me - place - offset + n, n) // apart

    def owned(ahead):
        first = lax.rem(me - place + ahead * apart - offset + n, n) // apart * cols
        return pl.ds(pl.multiple_of(first, cols), cols)

    def to_owners(send, keep):
        for ahead in reversed(range(OWNERS)):
            if ahead > 0:
                for copy in send(ahead, ahead * apart - place + n, lax.rem(place - ahead * apart + n, n)):
                    copy.start()
            else:

                @pl.when(place > 0)
                def _():
                    for copy in send(0, n - place, place):
                        copy.start()

                @pl.when(owner)
                def _():
                    keep()

    def sent_to_owners(send):
        for ahead in range(1, OWNERS):
            for copy in send(ahead, ahead * apart - place + n, lax.rem(place - ahead * apart + n, n)):
                copy.wait_send()

        @pl.when(place > 0)
        def _():
            for copy in send(0, n - place, place):
                copy.wait_send()

    def far_first(i):
        return n // 2 + (1 - 2 * (i % 2)) * ((i + 1) // 2)

    def sends(make):
        def body(i, carry):
            make(far_first(i)).start()
            return carry

        lax.fori_loop(0, n - 1, body, 0)

    def remote(src, dst, send, got, d):
        return pltpu.make_async_remote_copy(
            src_ref=src, dst_ref=dst, send_sem=send, recv_sem=got, device_id=peer(d), device_id_type=MESH
        )

    barrier = pltpu.get_barrier_semaphore()

    def greet(d, carry):
        pl.semaphore_signal(barrier, inc=1, device_id=peer(d), device_id_type=MESH)
        return carry

    lax.fori_loop(1, n, greet, 0)

    loads = [
        pltpu.make_async_copy(src, dst, load_sem.at[2 + i])
        for i, (src, dst) in enumerate(((ref_hbm, ref_ref), (pool_hbm, pool_ref), (kept_hbm, kept_ref)))
    ]
    for load in loads:
        load.start()
    load_keys = pltpu.make_async_copy(keys_hbm.at[0], keys, load_sem.at[0])
    load_vals = pltpu.make_async_copy(vals_hbm.at[0], vals, load_sem.at[1])
    load_keys.start()
    load_vals.start()

    for load in loads:
        load.wait()
    wanted = ref_ref[...] - me * pool_ref.shape[1]
    hit = lax.broadcasted_iota(jnp.int32, (pool_ref.shape[1], queries), 0) == wanted
    hit_t = jnp.where(hit, 1.0, 0.0).astype(F32).T.astype(BF16)
    q_part[...] = nn(hit_t, pool_ref[0]).astype(BF16)

    local = kept_ref[...] - me * rows
    local_col = jnp.broadcast_to(local, (128, kept)).T
    step = 512

    def chosen(i):
        base = lax.broadcasted_iota(jnp.int32, (kept, 128), 1) + i * step
        return jnp.concatenate(
            [jnp.where(local_col == base + 128 * j, 1.0, 0.0).astype(BF16) for j in range(step // 128)], axis=1
        )

    load_keys.wait()

    def pick_keys(i, carry):
        return carry + nn(chosen(i), keys[pl.ds(pl.multiple_of(i * step, step), step), :])

    kk_own[...] = lax.fori_loop(0, rows // step, pick_keys, jnp.zeros((kept, head), F32)).astype(BF16)

    def send_kept(ahead, d, slot):
        return (remote(kk_own, kk.at[slot], kept_send.at[ahead], kept_got.at[slot], d),)

    def keep_kept():
        kk[0] = kk_own[...]

    def send_vals(ahead, d, slot):
        return (remote(v_t.at[owned(ahead)], v_recv.at[slot], v_send.at[ahead], v_got, d),)

    def keep_vals():
        v_recv[0] = v_t[owned(0), :]

    pl.semaphore_wait(barrier, n - 1)

    for h in range(HALVES):

        def send_share(d, h=h):
            own = pl.ds(pl.multiple_of(h * half + lax.rem(me + d, n) * blk, blk), blk)
            return remote(q_part.at[own], q_recv.at[h, d], q_send.at[h], q_got.at[h], d)

        sends(send_share)
        mine = pl.ds(pl.multiple_of(h * half + me * blk, blk), blk)
        q_recv[h, 0] = q_part[mine, :]


    load_vals.wait()

    def pick_vals(i, carry):
        at = pl.ds(pl.multiple_of(i * step, step), step)
        vals_t[:, at] = vals[at, :].astype(F32).T.astype(BF16)
        return carry + nn(chosen(i), vals[at, :])

    kept_vals = lax.fori_loop(0, rows // step, pick_vals, jnp.zeros((kept, head), F32))
    vals_own[...] = kept_vals
    v_t[...] = kept_vals.T.astype(BF16)

    for h in range(HALVES):
        got = q_recv.at[h, pl.ds(1, n - 1)]
        pltpu.make_async_copy(got, got, q_got.at[h]).wait()
        total = q_recv[h, 0].astype(F32)
        for d in range(1, n):
            total = total + q_recv[h, d].astype(F32)
        q_blk[h] = total.astype(BF16)
        mine = pl.ds(pl.multiple_of(h * half + me * blk, blk), blk)

        def send_block(d, h=h, mine=mine):
            return remote(q_blk.at[h], q_all.at[mine], g_send.at[h], g_got.at[h], d)

        sends(send_block)
        q_all[mine, :] = q_blk[h]


    @pl.when(core == 0)
    def _():
        to_owners(send_kept, keep_kept)


    def near_target(h, d, slot):
        return (
            remote(stats.at[h], stats_near.at[h, slot], st_send.at[h], st_got.at[h, slot], d),
            remote(p_t.at[h], p_near.at[h, slot], p_send.at[h], p_got.at[h, slot], d),
        )

    span = min(rows, 2048)

    def attention(h, carry):
        got = q_all.at[pl.ds(0, (n - 1) * blk)]
        pltpu.make_async_copy(got, got, g_got.at[h]).wait()

        @pl.when((h == 0) & (core == 1))
        def _():
            to_owners(send_kept, keep_kept)

        @pl.when(h == 1)
        def _():
            to_owners(send_vals, keep_vals)

        q_turned = q_all[pl.ds(pl.multiple_of(h * half, half), half), :].astype(F32).T.astype(BF16)

        def score(i, top):
            at = pl.ds(pl.multiple_of(i * span, span), span)
            s = nn(keys[at, :], q_turned) * scale
            s_buf[at, :] = s
            return jnp.maximum(top, jnp.max(s.reshape(span // 8, 8, half), axis=0))

        top = lax.fori_loop(0, rows // span, score, jnp.full((8, half), -jnp.inf, F32))
        top = jnp.max(top, axis=0, keepdims=True)

        def weigh(i, carry):
            at = pl.ds(pl.multiple_of(i * span, span), span)
            e = jnp.exp(s_buf[at, :] - top)
            total = carry[0] + jnp.sum(e.reshape(span // 8, 8, half), axis=0)
            return total, carry[1] + nn(vals_t[:, at], e.astype(BF16))

        total, weighted = lax.fori_loop(
            0, rows // span, weigh, (jnp.zeros((8, half), F32), jnp.zeros((head, half), F32))
        )
        total = jnp.sum(total, axis=0, keepdims=True)
        p_t[h] = weighted
        lanes = [slice(j * 128, (j + 1) * 128) for j in range(half // 128)]
        stats[h] = jnp.concatenate([top[:, at] for at in lanes] + [total[:, at] for at in lanes], axis=0)
        for where, d, slot in ((1, n - 1, 1), (3, 1, 2), (2, n - 2 + 4 * h, 3)):

            @pl.when(seat == where)
            def _(d=d, slot=slot):
                for copy in near_target(h, d, slot):
                    copy.start()

        return carry

    lax.fori_loop(0, HALVES, attention, 0)

    def columns_at(d):
        return pl.ds(pl.multiple_of(lax.rem(me + d - offset + 2 * n, n) // apart * cols, cols), cols)

    below, above = (n - place, place // NEAR), (apart - place, place // NEAR + 2)

    def far_target(h, route):
        d, slot = route
        return (
            remote(stats_sum.at[h], stats_recv.at[h, slot], sts_send.at[h, slot], sts_got.at[h, slot], d),
            remote(p_sum.at[h, columns_at(d)], p_recv.at[h, slot], ps_send.at[h, slot], ps_got.at[h, slot], d),
        )

    def merge_near(h):
        for slot in (1, 2, 3):
            for copy in near_target(h, 1, slot):
                copy.wait_recv()
        for j in range(half // 128):
            lanes = slice(j * 128, (j + 1) * 128)
            tops = [stats[h, j : j + 1, :]] + [stats_near[h, slot, j : j + 1, :] for slot in (1, 2, 3)]
            best = functools.reduce(jnp.maximum, tops)
            factors = [jnp.exp(top - best) for top in tops]
            total = factors[0] * stats[h, 2 + j : 3 + j, :]
            weighted = factors[0] * p_t[h, :, lanes]
            for slot in (1, 2, 3):
                total = total + factors[slot] * stats_near[h, slot, 2 + j : 3 + j, :]
                weighted = weighted + factors[slot] * p_near[h, slot, :, lanes]
            stats_sum[h, j : j + 1, :] = best
            stats_sum[h, 2 + j : 3 + j, :] = total
            p_sum[h, :, lanes] = weighted

    @pl.when(seat == 0)
    def _():
        for h in range(HALVES):
            merge_near(h)
            for route in (below, above):
                for copy in far_target(h, route):
                    copy.start()

    @pl.when(owner)
    def _():
        q_now = q_all[...]
        top_buf[...] = jnp.full(top_buf.shape, -jnp.inf, F32)

        def kept_scores(first, count):
            wide = pl.ds(pl.multiple_of(first * kept, kept), count * kept)
            s = nt(q_now, kk[pl.ds(first, count)].reshape(count * kept, head)) * scale
            a_buf[:, wide] = s
            best = top_buf[...]
            for j in range(count * kept // 128):
                best = jnp.maximum(best, s[:, j * 128 : (j + 1) * 128])
            top_buf[...] = best

        def arrived(i, carry):
            first = i // 2 * NEAR + i % 2 * (n - NEAR - i // 2 * 2 * NEAR)
            for j in range(NEAR):

                @pl.when(first + j > 0)
                def _(j=j):
                    slot = kk.at[first + j]
                    pltpu.make_async_copy(slot, slot, kept_got.at[first + j]).wait()

            kept_scores(first, NEAR)
            return carry

        lax.fori_loop(0, n // NEAR, arrived, 0)
        best = jnp.max(top_buf[...], axis=1, keepdims=True)
        top_buf[...] = jnp.broadcast_to(best, top_buf.shape)

        def kept_weights(i, carry):
            at = pl.ds(pl.multiple_of(i * 1024, 1024), 1024)
            for r in range(0, queries, 16):
                some = slice(r, r + 16)
                top = jnp.concatenate([top_buf[some, :]] * 8, axis=1)
                high, low = split(jnp.exp(a_buf[some, at] - top))
                a_both[0, some, at] = high
                a_both[1, some, at] = low + low
            return carry

        lax.fori_loop(0, n * kept // 1024, kept_weights, 0)

        wide = queries // 2
        gram[0, :wide, :wide] = nt(a_both[0, :wide, :], a_both[0, :wide, :])
        gram[0, wide:queries, :wide] = jnp.zeros((queries - wide, wide), F32)
        right = nt(a_both[0, :queries, :], a_both[0, wide:queries, :])
        gram[0, :wide, wide:] = right[:wide] + right[:wide]
        gram[0, wide:queries, wide:] = right[wide:]

        got = v_recv.at[pl.ds(1, n - 1)]
        pltpu.make_async_copy(got, got, v_got).wait()
        for d in range(n):
            a_both[0, queries : queries + cols, d * kept : (d + 1) * kept] = v_recv[d]
        a_both[0, queries + cols :, :] = jnp.ones((16, n * kept), BF16)

        def products(i, carry):
            at = pl.ds(pl.multiple_of(i * wide, wide), wide)
            gram[1, :, at] = nt(a_both[0], a_both[1, at, :])
            return carry

        lax.fori_loop(0, queries // wide, products, 0)
        sums = nt(a_both[0, queries:, :], a_both[0, :queries, :]) + 0.5 * gram[1, queries:, :]
        inverse = 1.0 / sums[cols : cols + 1, :]
        fitted_now = sums[:cols, :] * inverse
        once = gram[0, :queries, :] + gram[1, :queries, :]
        gram_high, gram_low = split(0.5 * (once + once.T))

        pieces = []
        for h in range(HALVES):
            for slot in range(4):
                for copy in far_target(h, (NEAR, slot)):
                    copy.wait_recv()
            for j in range(half // 128):
                tops = stats_recv[h, :, j : j + 1, :]
                totals = stats_recv[h, :, 2 + j : 3 + j, :]
                factor = jnp.exp(tops - jnp.max(tops, axis=0, keepdims=True))
                weighted = jnp.sum(factor * p_recv[h, :, :, j * 128 : (j + 1) * 128], axis=0)
                pieces.append(weighted / jnp.sum(factor * totals, axis=0))
        target = jnp.concatenate(pieces, axis=1)

        def apply(x):
            high, low = split(x * inverse)
            both = nn(jnp.concatenate([high, low], axis=0), gram_high)
            return (both[:cols] + both[cols:] + nn(high, gram_low)) * inverse

        def dots(a, b):
            return jnp.sum(a * b, axis=1, keepdims=True)

        y = target - fitted_now
        image_y = apply(y)
        norm_now = dots(y, image_y)
        u, image = y, image_y
        answer = jnp.zeros_like(y)
        for it in range(ITERS):
            curve = dots(image, image) + ridge * dots(u, image)
            alpha = norm_now / curve
            answer = answer + alpha * u
            if it == ITERS - 1:
                break
            y = y - alpha * (image + ridge * u)
            image_y = apply(y)
            norm_next = dots(y, image_y)
            beta = norm_next / norm_now
            u = y + beta * u
            image = image_y + beta * image
            norm_now = norm_next

        high, low = split(answer * inverse)
        both_ways = jnp.concatenate([high, low], axis=0)

        def give(first):
            at = pl.ds(pl.multiple_of(first * kept, 2 * kept), 2 * kept)
            both = nn(both_ways, a_both[0, :queries, at])
            change = both[:cols] + both[cols:] + 0.5 * nn(high, a_both[1, :queries, at])
            largest = jnp.max(jnp.abs(change), axis=0, keepdims=True)
            factor = jnp.where(largest > 1e-30, 32767.0 / jnp.maximum(largest, 1e-30), 0.0)
            codes = jnp.round(change * factor).astype(jnp.int32).astype(jnp.int16)
            unit = largest * (1.0 / 32767.0)
            for j in range(2):
                d = first + j
                res[d] = codes[:, j * kept : (j + 1) * kept]
                units[d] = jnp.concatenate(
                    [unit[:, j * kept + k * 128 : j * kept + (k + 1) * 128] for k in range(kept // 128)], axis=0
                )

                @pl.when(d > 0)
                def _(d=d):
                    remote(res.at[d], fin.at[owned(0)], f_send, f_got, d).start()
                    remote(units.at[d], fin_units.at[column_block], u_send, u_got, d).start()

        def give_pairs(i, carry):
            give(n // 2 + 2 * i)
            give(n // 2 - 2 - 2 * i)
            return carry

        lax.fori_loop(0, n // 4, give_pairs, 0)
        fin[owned(0), :] = res[0]
        fin_units[column_block] = units[0]

    def drain(ref, sem):
        pltpu.make_async_copy(ref, ref, sem).wait()

    for h in range(HALVES):
        drain(q_recv.at[h, pl.ds(1, n - 1)], q_send.at[h])
        drain(q_all.at[pl.ds(0, (n - 1) * blk)], g_send.at[h])
    sent_to_owners(send_vals)
    sent_to_owners(send_kept)

    @pl.when(owner)
    def _():
        drain(res.at[pl.ds(1, n - 1)], f_send)
        drain(units.at[pl.ds(1, n - 1)], u_send)
        drain(fin.at[pl.ds(0, head - cols)], f_got)
        drain(fin_units.at[pl.ds(0, OWNERS - 1)], u_got)

    @pl.when(seat == 0)
    def _():
        for h in range(HALVES):
            for route in (below, above):
                for copy in far_target(h, route):
                    copy.wait_send()

    @pl.when(seat > 0)
    def _():
        for h in range(HALVES):
            for copy in near_target(h, 1, 1):
                copy.wait_send()

    @pl.when(place > 0)
    def _():
        drain(fin, f_got)
        drain(fin_units, u_got)

    for j in range(OWNERS):
        at = slice(j * cols, (j + 1) * cols)
        unit = jnp.concatenate([fin_units[j, k : k + 1, :] for k in range(kept // 128)], axis=1)
        turned[at, :] = fin[at, :].astype(jnp.int32).astype(F32) * unit
    out_ref[0] = vals_own[...] + turned[...].T


def local(cache_keys, cache_values, query_pool, kept_index, ref_index):
    n = lax.axis_size("ctx")
    rows, head = cache_keys.shape[1:]
    kept = kept_index.shape[1]
    pool = query_pool.shape[1]
    queries = ref_index.shape[1]
    half = queries // HALVES
    blk = half // n
    cols = head // OWNERS
    vmem = pl.BlockSpec(memory_space=pltpu.VMEM)
    hbm = pl.BlockSpec(memory_space=pl.ANY)
    dma = pltpu.SemaphoreType.DMA
    return pl.pallas_call(
        functools.partial(kernel, n),
        out_shape=jax.ShapeDtypeStruct((1, kept, head), F32),
        in_specs=[hbm] * 5,
        out_specs=vmem,
        scratch_shapes=[
            pltpu.VMEM((1, pool, head), BF16),
            pltpu.VMEM((1, kept), jnp.int32),
            pltpu.VMEM((1, queries), jnp.int32),
            pltpu.VMEM((rows, head), BF16),
            pltpu.VMEM((rows, head), BF16),
            pltpu.VMEM((head, rows), BF16),
            pltpu.VMEM((queries, head), BF16),
            pltpu.VMEM((HALVES, n, blk, head), BF16),
            pltpu.VMEM((HALVES, blk, head), BF16),
            pltpu.VMEM((queries, head), BF16),
            pltpu.VMEM((kept, head), BF16),
            pltpu.VMEM((n, kept, head), BF16),
            pltpu.VMEM((head, kept), BF16),
            pltpu.VMEM((n, cols, kept), BF16),
            pltpu.VMEM((rows, half), F32),
            pltpu.VMEM((HALVES, head, half), F32),
            pltpu.VMEM((HALVES, 4, 128), F32),
            pltpu.VMEM((HALVES, 4, head, half), F32),
            pltpu.VMEM((HALVES, 4, 4, 128), F32),
            pltpu.VMEM((HALVES, head, half), F32),
            pltpu.VMEM((HALVES, 4, 128), F32),
            pltpu.VMEM((HALVES, 4, cols, half), F32),
            pltpu.VMEM((HALVES, 4, 4, 128), F32),
            pltpu.VMEM((queries, n * kept), F32),
            pltpu.VMEM((queries, 128), F32),
            pltpu.VMEM((2, queries + cols + 16, n * kept), BF16),
            pltpu.VMEM((2, queries + cols + 16, queries), F32),
            pltpu.VMEM((n, cols, kept), jnp.int16),
            pltpu.VMEM((head, kept), jnp.int16),
            pltpu.VMEM((n, kept // 128, 128), F32),
            pltpu.VMEM((OWNERS, kept // 128, 128), F32),
            pltpu.VMEM((head, kept), F32),
            pltpu.VMEM((kept, head), F32),
            dma((5,)),
            dma((HALVES,)),
            dma((HALVES,)),
            dma((HALVES,)),
            dma((HALVES,)),
            dma((OWNERS,)),
            dma((n,)),
            dma((OWNERS,)),
            dma,
            dma((HALVES,)),
            dma((HALVES, 4)),
            dma((HALVES,)),
            dma((HALVES, 4)),
            dma((HALVES, 4)),
            dma((HALVES, 4)),
            dma((HALVES, 4)),
            dma((HALVES, 4)),
            dma,
            dma,
            dma,
            dma,
        ],
        compiler_params=pltpu.CompilerParams(
            collective_id=0, has_side_effects=True, vmem_limit_bytes=56 * 1024 * 1024
        ),
    )(cache_keys, cache_values, query_pool, kept_index, ref_index)


def solution(mesh):
    placed = (
        P("rep", "ctx", None),
        P("rep", "ctx", None),
        P("rep", "ctx", None),
        P("rep", "ctx"),
        P("rep", None),
    )
    return jax.shard_map(
        local, mesh=mesh, in_specs=placed, out_specs=P("rep", "ctx", None), check_vma=False
    )
```

```python
import functools

import jax
import jax.numpy as jnp
from jax import lax
from jax.experimental import pallas as pl
from jax.experimental.pallas import tpu as pltpu
from jax.sharding import PartitionSpec as P

ITERS = 3
HALVES = 2
OWNERS = 2
NEAR = 4
F32 = jnp.float32
BF16 = jnp.bfloat16
MESH = pl.DeviceIdType.MESH


def nt(a, b):
    return lax.dot_general(a, b, (((1,), (1,)), ((), ())), preferred_element_type=F32)


def nn(a, b):
    return lax.dot_general(a, b, (((1,), (0,)), ((), ())), preferred_element_type=F32)


def split(x):
    high = x.astype(BF16)
    return high, (x - high.astype(F32)).astype(BF16)


def kernel(
    n, keys_hbm, vals_hbm, pool_hbm, kept_hbm, ref_hbm, out_ref,
    pool_ref, kept_ref, ref_ref,
    keys, vals, vals_t, q_part, q_recv, q_blk, q_all, kk_own, kk, v_t, v_recv,
    s_buf, p_t, stats, p_near, stats_near, p_sum, stats_sum, p_recv, stats_recv, a_buf, top_buf, a_both, gram, res, fin, units, fin_units, turned, vals_own,
    load_sem, q_send, q_got, g_send, g_got, kept_send, kept_got, v_send, v_got,
    p_send, p_got, st_send, st_got, ps_send, ps_got, sts_send, sts_got, f_send, f_got, u_send, u_got,
):
    me = lax.axis_index("ctx")
    rows, head = keys.shape
    kept = kk.shape[1]
    queries = q_all.shape[0]
    half = queries // HALVES
    blk = half // n
    cols = head // OWNERS
    apart = n // OWNERS
    scale = 1.0 / head**0.5
    ridge = 0.3 * queries / ((kept * n) * (kept * n))

    def peer(d):
        return {"ctx": lax.rem(me + d, n)}

    core = lax.rem(lax.axis_index("rep"), 2)
    offset = core * (apart // 2)
    place = lax.rem(me - offset + n, apart)
    owner = place == 0
    seat = lax.rem(place + NEAR - 1 - 2 * core, NEAR)

    column_block = lax.rem(me - place - offset + n, n) // apart

    def owned(ahead):
        first = lax.rem(me - place + ahead * apart - offset + n, n) // apart * cols
        return pl.ds(pl.multiple_of(first, cols), cols)

    def to_owners(send, keep):
        for ahead in reversed(range(OWNERS)):
            if ahead > 0:
                for copy in send(ahead, ahead * apart - place + n, lax.rem(place - ahead * apart + n, n)):
                    copy.start()
            else:

                @pl.when(place > 0)
                def _():
                    for copy in send(0, n - place, place):
                        copy.start()

                @pl.when(owner)
                def _():
                    keep()

    def sent_to_owners(send):
        for ahead in range(1, OWNERS):
            for copy in send(ahead, ahead * apart - place + n, lax.rem(place - ahead * apart + n, n)):
                copy.wait_send()

        @pl.when(place > 0)
        def _():
            for copy in send(0, n - place, place):
                copy.wait_send()

    def far_first(i):
        return n // 2 + (1 - 2 * (i % 2)) * ((i + 1) // 2)

    def sends(make):
        def body(i, carry):
            make(far_first(i)).start()
            return carry

        lax.fori_loop(0, n - 1, body, 0)

    def remote(src, dst, send, got, d):
        return pltpu.make_async_remote_copy(
            src_ref=src, dst_ref=dst, send_sem=send, recv_sem=got, device_id=peer(d), device_id_type=MESH
        )

    barrier = pltpu.get_barrier_semaphore()

    def greet(i, carry):
        pl.semaphore_signal(barrier, inc=1, device_id=peer(far_first(i)), device_id_type=MESH)
        return carry

    lax.fori_loop(0, n - 1, greet, 0)

    loads = [
        pltpu.make_async_copy(src, dst, load_sem.at[2 + i])
        for i, (src, dst) in enumerate(((ref_hbm, ref_ref), (pool_hbm, pool_ref), (kept_hbm, kept_ref)))
    ]
    for load in loads:
        load.start()
    load_keys = pltpu.make_async_copy(keys_hbm.at[0], keys, load_sem.at[0])
    load_vals = pltpu.make_async_copy(vals_hbm.at[0], vals, load_sem.at[1])
    load_keys.start()
    load_vals.start()

    for load in loads:
        load.wait()
    wanted = ref_ref[...] - me * pool_ref.shape[1]
    hit = lax.broadcasted_iota(jnp.int32, (pool_ref.shape[1], queries), 0) == wanted
    hit_t = jnp.where(hit, 1.0, 0.0).astype(F32).T.astype(BF16)
    q_part[...] = nn(hit_t, pool_ref[0]).astype(BF16)

    local = kept_ref[...] - me * rows
    local_col = jnp.broadcast_to(local, (128, kept)).T
    step = 512

    def chosen(i):
        base = lax.broadcasted_iota(jnp.int32, (kept, 128), 1) + i * step
        return jnp.concatenate(
            [jnp.where(local_col == base + 128 * j, 1.0, 0.0).astype(BF16) for j in range(step // 128)], axis=1
        )

    load_keys.wait()

    def pick_keys(i, carry):
        return carry + nn(chosen(i), keys[pl.ds(pl.multiple_of(i * step, step), step), :])

    kk_own[...] = lax.fori_loop(0, rows // step, pick_keys, jnp.zeros((kept, head), F32)).astype(BF16)

    def send_kept(ahead, d, slot):
        return (remote(kk_own, kk.at[slot], kept_send.at[ahead], kept_got.at[slot], d),)

    def keep_kept():
        kk[0] = kk_own[...]

    def send_vals(ahead, d, slot):
        return (remote(v_t.at[owned(ahead)], v_recv.at[slot], v_send.at[ahead], v_got, d),)

    def keep_vals():
        v_recv[0] = v_t[owned(0), :]

    pl.semaphore_wait(barrier, n - 1)

    for h in range(HALVES):

        def send_share(d, h=h):
            own = pl.ds(pl.multiple_of(h * half + lax.rem(me + d, n) * blk, blk), blk)
            return remote(q_part.at[own], q_recv.at[h, d], q_send.at[h], q_got.at[h], d)

        sends(send_share)
        mine = pl.ds(pl.multiple_of(h * half + me * blk, blk), blk)
        q_recv[h, 0] = q_part[mine, :]


    load_vals.wait()

    def pick_vals(i, carry):
        at = pl.ds(pl.multiple_of(i * step, step), step)
        vals_t[:, at] = vals[at, :].astype(F32).T.astype(BF16)
        return carry + nn(chosen(i), vals[at, :])

    kept_vals = lax.fori_loop(0, rows // step, pick_vals, jnp.zeros((kept, head), F32))
    vals_own[...] = kept_vals
    v_t[...] = kept_vals.T.astype(BF16)

    for h in range(HALVES):
        got = q_recv.at[h, pl.ds(1, n - 1)]
        pltpu.make_async_copy(got, got, q_got.at[h]).wait()
        total = q_recv[h, 0].astype(F32)
        for d in range(1, n):
            total = total + q_recv[h, d].astype(F32)
        q_blk[h] = total.astype(BF16)
        mine = pl.ds(pl.multiple_of(h * half + me * blk, blk), blk)

        def send_block(d, h=h, mine=mine):
            return remote(q_blk.at[h], q_all.at[mine], g_send.at[h], g_got.at[h], d)

        sends(send_block)
        q_all[mine, :] = q_blk[h]


    @pl.when(core == 0)
    def _():
        to_owners(send_kept, keep_kept)


    def near_target(h, d, slot):
        return (
            remote(stats.at[h], stats_near.at[h, slot], st_send.at[h], st_got.at[h, slot], d),
            remote(p_t.at[h], p_near.at[h, slot], p_send.at[h], p_got.at[h, slot], d),
        )

    span = min(rows, 2048)

    def attention(h, carry):
        got = q_all.at[pl.ds(0, (n - 1) * blk)]
        pltpu.make_async_copy(got, got, g_got.at[h]).wait()

        @pl.when((h == 0) & (core == 1))
        def _():
            to_owners(send_kept, keep_kept)

        @pl.when(h == core)
        def _():
            to_owners(send_vals, keep_vals)

        q_turned = q_all[pl.ds(pl.multiple_of(h * half, half), half), :].astype(F32).T.astype(BF16)

        def score(i, top):
            at = pl.ds(pl.multiple_of(i * span, span), span)
            s = nn(keys[at, :], q_turned) * scale
            s_buf[at, :] = s
            return jnp.maximum(top, jnp.max(s.reshape(span // 8, 8, half), axis=0))

        top = lax.fori_loop(0, rows // span, score, jnp.full((8, half), -jnp.inf, F32))
        top = jnp.max(top, axis=0, keepdims=True)

        def weigh(i, carry):
            at = pl.ds(pl.multiple_of(i * span, span), span)
            e = jnp.exp(s_buf[at, :] - top)
            total = carry[0] + jnp.sum(e.reshape(span // 8, 8, half), axis=0)
            return total, carry[1] + nn(vals_t[:, at], e.astype(BF16))

        total, weighted = lax.fori_loop(
            0, rows // span, weigh, (jnp.zeros((8, half), F32), jnp.zeros((head, half), F32))
        )
        total = jnp.sum(total, axis=0, keepdims=True)
        p_t[h] = weighted
        lanes = [slice(j * 128, (j + 1) * 128) for j in range(half // 128)]
        stats[h] = jnp.concatenate([top[:, at] for at in lanes] + [total[:, at] for at in lanes], axis=0)
        for where, d, slot in ((1, n - 1, 1), (3, 1, 2), (2, n - 2 + 4 * h, 3)):

            @pl.when(seat == where)
            def _(d=d, slot=slot):
                for copy in near_target(h, d, slot):
                    copy.start()

        return carry

    lax.fori_loop(0, HALVES, attention, 0)

    def columns_at(d):
        return pl.ds(pl.multiple_of(lax.rem(me + d - offset + 2 * n, n) // apart * cols, cols), cols)

    below, above = (n - place, place // NEAR), (apart - place, place // NEAR + 2)

    def far_target(h, route):
        d, slot = route
        return (
            remote(stats_sum.at[h], stats_recv.at[h, slot], sts_send.at[h, slot], sts_got.at[h, slot], d),
            remote(p_sum.at[h, columns_at(d)], p_recv.at[h, slot], ps_send.at[h, slot], ps_got.at[h, slot], d),
        )

    def merge_near(h):
        for slot in (1, 2, 3):
            for copy in near_target(h, 1, slot):
                copy.wait_recv()
        for j in range(half // 128):
            lanes = slice(j * 128, (j + 1) * 128)
            tops = [stats[h, j : j + 1, :]] + [stats_near[h, slot, j : j + 1, :] for slot in (1, 2, 3)]
            best = functools.reduce(jnp.maximum, tops)
            factors = [jnp.exp(top - best) for top in tops]
            total = factors[0] * stats[h, 2 + j : 3 + j, :]
            weighted = factors[0] * p_t[h, :, lanes]
            for slot in (1, 2, 3):
                total = total + factors[slot] * stats_near[h, slot, 2 + j : 3 + j, :]
                weighted = weighted + factors[slot] * p_near[h, slot, :, lanes]
            stats_sum[h, j : j + 1, :] = best
            stats_sum[h, 2 + j : 3 + j, :] = total
            p_sum[h, :, lanes] = weighted

    @pl.when(seat == 0)
    def _():
        for h in range(HALVES):
            merge_near(h)
            for route in (below, above):
                for copy in far_target(h, route):
                    copy.start()

    @pl.when(owner)
    def _():
        q_now = q_all[...]
        top_buf[...] = jnp.full(top_buf.shape, -jnp.inf, F32)

        def kept_scores(first, count):
            wide = pl.ds(pl.multiple_of(first * kept, kept), count * kept)
            s = nt(q_now, kk[pl.ds(first, count)].reshape(count * kept, head)) * scale
            a_buf[:, wide] = s
            best = top_buf[...]
            for j in range(count * kept // 128):
                best = jnp.maximum(best, s[:, j * 128 : (j + 1) * 128])
            top_buf[...] = best

        def arrived(i, carry):
            first = i // 2 * NEAR + i % 2 * (n - NEAR - i // 2 * 2 * NEAR)
            for j in range(NEAR):

                @pl.when(first + j > 0)
                def _(j=j):
                    slot = kk.at[first + j]
                    pltpu.make_async_copy(slot, slot, kept_got.at[first + j]).wait()

            kept_scores(first, NEAR)
            return carry

        lax.fori_loop(0, n // NEAR, arrived, 0)
        best = jnp.max(top_buf[...], axis=1, keepdims=True)
        top_buf[...] = jnp.broadcast_to(best, top_buf.shape)

        def kept_weights(i, carry):
            at = pl.ds(pl.multiple_of(i * 1024, 1024), 1024)
            for r in range(0, queries, 16):
                some = slice(r, r + 16)
                top = jnp.concatenate([top_buf[some, :]] * 8, axis=1)
                high, low = split(jnp.exp(a_buf[some, at] - top))
                a_both[0, some, at] = high
                a_both[1, some, at] = low + low
            return carry

        lax.fori_loop(0, n * kept // 1024, kept_weights, 0)

        wide = queries // 2
        gram[0, :wide, :wide] = nt(a_both[0, :wide, :], a_both[0, :wide, :])
        gram[0, wide:queries, :wide] = jnp.zeros((queries - wide, wide), F32)
        right = nt(a_both[0, :queries, :], a_both[0, wide:queries, :])
        gram[0, :wide, wide:] = right[:wide] + right[:wide]
        gram[0, wide:queries, wide:] = right[wide:]

        got = v_recv.at[pl.ds(1, n - 1)]
        pltpu.make_async_copy(got, got, v_got).wait()
        for d in range(n):
            a_both[0, queries : queries + cols, d * kept : (d + 1) * kept] = v_recv[d]
        a_both[0, queries + cols :, :] = jnp.ones((16, n * kept), BF16)

        def products(i, carry):
            at = pl.ds(pl.multiple_of(i * wide, wide), wide)
            gram[1, :, at] = nt(a_both[0], a_both[1, at, :])
            return carry

        lax.fori_loop(0, queries // wide, products, 0)
        sums = nt(a_both[0, queries:, :], a_both[0, :queries, :]) + 0.5 * gram[1, queries:, :]
        inverse = 1.0 / sums[cols : cols + 1, :]
        fitted_now = sums[:cols, :] * inverse
        once = gram[0, :queries, :] + gram[1, :queries, :]
        gram_high, gram_low = split(0.5 * (once + once.T))

        pieces = []
        for h in range(HALVES):
            for slot in range(4):
                for copy in far_target(h, (NEAR, slot)):
                    copy.wait_recv()
            for j in range(half // 128):
                tops = stats_recv[h, :, j : j + 1, :]
                totals = stats_recv[h, :, 2 + j : 3 + j, :]
                factor = jnp.exp(tops - jnp.max(tops, axis=0, keepdims=True))
                weighted = jnp.sum(factor * p_recv[h, :, :, j * 128 : (j + 1) * 128], axis=0)
                pieces.append(weighted / jnp.sum(factor * totals, axis=0))
        target = jnp.concatenate(pieces, axis=1)

        def apply(x):
            high, low = split(x * inverse)
            both = nn(jnp.concatenate([high, low], axis=0), gram_high)
            return (both[:cols] + both[cols:] + nn(high, gram_low)) * inverse

        def dots(a, b):
            return jnp.sum(a * b, axis=1, keepdims=True)

        y = target - fitted_now
        image_y = apply(y)
        norm_now = dots(y, image_y)
        u, image = y, image_y
        answer = jnp.zeros_like(y)
        for it in range(ITERS):
            curve = dots(image, image) + ridge * dots(u, image)
            alpha = norm_now / curve
            answer = answer + alpha * u
            if it == ITERS - 1:
                break
            y = y - alpha * (image + ridge * u)
            image_y = apply(y)
            norm_next = dots(y, image_y)
            beta = norm_next / norm_now
            u = y + beta * u
            image = image_y + beta * image
            norm_now = norm_next

        high, low = split(answer * inverse)
        both_ways = jnp.concatenate([high, low], axis=0)

        def give(first):
            at = pl.ds(pl.multiple_of(first * kept, 2 * kept), 2 * kept)
            both = nn(both_ways, a_both[0, :queries, at])
            change = both[:cols] + both[cols:] + 0.5 * nn(high, a_both[1, :queries, at])
            largest = jnp.max(jnp.abs(change), axis=0, keepdims=True)
            factor = jnp.where(largest > 1e-30, 32767.0 / jnp.maximum(largest, 1e-30), 0.0)
            codes = jnp.round(change * factor).astype(jnp.int32).astype(jnp.int16)
            unit = largest * (1.0 / 32767.0)
            for j in range(2):
                d = first + j
                res[d] = codes[:, j * kept : (j + 1) * kept]
                units[d] = jnp.concatenate(
                    [unit[:, j * kept + k * 128 : j * kept + (k + 1) * 128] for k in range(kept // 128)], axis=0
                )

                @pl.when(d > 0)
                def _(d=d):
                    remote(res.at[d], fin.at[owned(0)], f_send, f_got, d).start()
                    remote(units.at[d], fin_units.at[column_block], u_send, u_got, d).start()

        def give_pairs(i, carry):
            give(n // 2 + 2 * i)
            give(n // 2 - 2 - 2 * i)
            return carry

        lax.fori_loop(0, n // 4, give_pairs, 0)
        fin[owned(0), :] = res[0]
        fin_units[column_block] = units[0]

    def drain(ref, sem):
        pltpu.make_async_copy(ref, ref, sem).wait()

    for h in range(HALVES):
        drain(q_recv.at[h, pl.ds(1, n - 1)], q_send.at[h])
        drain(q_all.at[pl.ds(0, (n - 1) * blk)], g_send.at[h])
    sent_to_owners(send_vals)
    sent_to_owners(send_kept)

    @pl.when(owner)
    def _():
        drain(res.at[pl.ds(1, n - 1)], f_send)
        drain(units.at[pl.ds(1, n - 1)], u_send)
        drain(fin.at[pl.ds(0, head - cols)], f_got)
        drain(fin_units.at[pl.ds(0, OWNERS - 1)], u_got)

    @pl.when(seat == 0)
    def _():
        for h in range(HALVES):
            for route in (below, above):
                for copy in far_target(h, route):
                    copy.wait_send()

    @pl.when(seat > 0)
    def _():
        for h in range(HALVES):
            for copy in near_target(h, 1, 1):
                copy.wait_send()

    @pl.when(place > 0)
    def _():
        drain(fin, f_got)
        drain(fin_units, u_got)

    for j in range(OWNERS):
        at = slice(j * cols, (j + 1) * cols)
        unit = jnp.concatenate([fin_units[j, k : k + 1, :] for k in range(kept // 128)], axis=1)
        turned[at, :] = fin[at, :].astype(jnp.int32).astype(F32) * unit
    out_ref[0] = vals_own[...] + turned[...].T


def local(cache_keys, cache_values, query_pool, kept_index, ref_index):
    n = lax.axis_size("ctx")
    rows, head = cache_keys.shape[1:]
    kept = kept_index.shape[1]
    pool = query_pool.shape[1]
    queries = ref_index.shape[1]
    half = queries // HALVES
    blk = half // n
    cols = head // OWNERS
    vmem = pl.BlockSpec(memory_space=pltpu.VMEM)
    hbm = pl.BlockSpec(memory_space=pl.ANY)
    dma = pltpu.SemaphoreType.DMA
    return pl.pallas_call(
        functools.partial(kernel, n),
        out_shape=jax.ShapeDtypeStruct((1, kept, head), F32),
        in_specs=[hbm] * 5,
        out_specs=vmem,
        scratch_shapes=[
            pltpu.VMEM((1, pool, head), BF16),
            pltpu.VMEM((1, kept), jnp.int32),
            pltpu.VMEM((1, queries), jnp.int32),
            pltpu.VMEM((rows, head), BF16),
            pltpu.VMEM((rows, head), BF16),
            pltpu.VMEM((head, rows), BF16),
            pltpu.VMEM((queries, head), BF16),
            pltpu.VMEM((HALVES, n, blk, head), BF16),
            pltpu.VMEM((HALVES, blk, head), BF16),
            pltpu.VMEM((queries, head), BF16),
            pltpu.VMEM((kept, head), BF16),
            pltpu.VMEM((n, kept, head), BF16),
            pltpu.VMEM((head, kept), BF16),
            pltpu.VMEM((n, cols, kept), BF16),
            pltpu.VMEM((rows, half), F32),
            pltpu.VMEM((HALVES, head, half), F32),
            pltpu.VMEM((HALVES, 4, 128), F32),
            pltpu.VMEM((HALVES, 4, head, half), F32),
            pltpu.VMEM((HALVES, 4, 4, 128), F32),
            pltpu.VMEM((HALVES, head, half), F32),
            pltpu.VMEM((HALVES, 4, 128), F32),
            pltpu.VMEM((HALVES, 4, cols, half), F32),
            pltpu.VMEM((HALVES, 4, 4, 128), F32),
            pltpu.VMEM((queries, n * kept), F32),
            pltpu.VMEM((queries, 128), F32),
            pltpu.VMEM((2, queries + cols + 16, n * kept), BF16),
            pltpu.VMEM((2, queries + cols + 16, queries), F32),
            pltpu.VMEM((n, cols, kept), jnp.int16),
            pltpu.VMEM((head, kept), jnp.int16),
            pltpu.VMEM((n, kept // 128, 128), F32),
            pltpu.VMEM((OWNERS, kept // 128, 128), F32),
            pltpu.VMEM((head, kept), F32),
            pltpu.VMEM((kept, head), F32),
            dma((5,)),
            dma((HALVES,)),
            dma((HALVES,)),
            dma((HALVES,)),
            dma((HALVES,)),
            dma((OWNERS,)),
            dma((n,)),
            dma((OWNERS,)),
            dma,
            dma((HALVES,)),
            dma((HALVES, 4)),
            dma((HALVES,)),
            dma((HALVES, 4)),
            dma((HALVES, 4)),
            dma((HALVES, 4)),
            dma((HALVES, 4)),
            dma((HALVES, 4)),
            dma,
            dma,
            dma,
            dma,
        ],
        compiler_params=pltpu.CompilerParams(
            collective_id=0, has_side_effects=True, vmem_limit_bytes=56 * 1024 * 1024
        ),
    )(cache_keys, cache_values, query_pool, kept_index, ref_index)


def solution(mesh):
    placed = (
        P("rep", "ctx", None),
        P("rep", "ctx", None),
        P("rep", "ctx", None),
        P("rep", "ctx"),
        P("rep", None),
    )
    return jax.shard_map(
        local, mesh=mesh, in_specs=placed, out_specs=P("rep", "ctx", None), check_vma=False
    )
```
